32 devices in a mesh: dp: 4 (over y, core), seq: 8 (over z, x).
Axes of the slice: x: 2, y: 2, z: 4, core: 2. Of those that a mesh axis runs over, the one named last changes fastest.
Arguments:
- tokens: bfloat16 [4096, 1024], P(('dp', 'seq')), may hold values from -6 to 6
- gate_values: float32 [4096, 2], P(('dp', 'seq')), may hold values from 0.2 to 1
- expert_ids: int32 [4096, 2], P(('dp', 'seq')), may hold values from 0 to 31, all different within a row; in each aligned block of 128 rows (0 to 127, 128 to 255, ...) at most 9 rows name the same one
- cotangent: bfloat16 [4096, 1024], P(('dp', 'seq')), may hold values from -6 to 6
- weight_in: bfloat16 [32768, 1024], P('seq'), may hold values from -0.1875 to 0.1875
- weight_out: bfloat16 [32768, 1024], P('seq'), may hold values from -0.1875 to 0.1875
Outputs:
- layer_out: bfloat16 [4096, 1024], P(('dp', 'seq'))
- gate_grad: float32 [4096, 2], P(('dp', 'seq'))
- input_grad: bfloat16 [4096, 1024], P(('dp', 'seq'))
- weight_in_grad: float32 [1024, 32768], P('dp', 'seq')
- weight_out_grad: float32 [1024, 32768], P('dp', 'seq')
The draws below stay inside these ranges and needn't reach their ends.
Inputs may be any that keep to these rules, and one draw needn't show every extreme that they name: `expert_ids`: each row names two different experts; within the rows of one device no expert is named more than 9 times, a bound that some block reaches.
All inputs are finite; a program needn't handle non-finite values.
Results may differ from the reference program's by a relative error of at most 0.017.
Values may be sent and summed in bfloat16 or wider, within the bound.
No kernel may reach another device: no remote copies, remote signals or barrier semaphores. Data moves between devices by JAX's collectives and lax.ppermute only.
A program may use at most 128 MiB of HBM per device.

```python
import math
import jax
import jax.numpy as jnp
import numpy as np
from jax import lax

D = 1024
E = 32
FF = 1024
TOK_DEV = 128
TOKENS = 4096
CAP = 9
BLOCK_UNITS = 1024
BLOCKS = 1
N_DP = 4
N_SEQ = 8


def shard_levels(rng, dims, shards, low, top_value):
    level, own = 1.0, jax.random.fold_in(rng, 6)
    for position, blocks in shards:
        draws = jnp.exp(jax.random.uniform(jax.random.fold_in(own, position), (blocks,), jnp.float32, low / len(shards), top_value / len(shards)))
        level = level * jnp.repeat(draws, dims[position] // blocks).reshape([-1 if axis == position else 1 for axis in range(len(dims))])
    return level


def assign_block(stream_key, own, number, rows, amount, top, most, skew):
    order = jax.random.permutation(stream_key, amount)
    crowded, usual = portions_of(amount, rows * top, most, skew, True), portions_of(amount, rows * top, most, skew, False)
    places = jnp.arange(amount)

    def named(sizes, rotation):
        used = int((sizes > 0).sum())
        fixed = max(1, used // 4)
        passed = fixed + (places - fixed + rotation * (used - fixed)) % max(1, amount - fixed)
        return jnp.zeros((amount,), jnp.int32).at[order[jnp.where(places < fixed, places, passed)]].set(jnp.asarray(sizes, jnp.int32))

    sizes = jnp.where(number % 4 == 0, named(crowded, number // 4), named(usual, number - number // 4 - 1))
    mixed = jax.random.permutation(jax.random.fold_in(own, 3), amount)
    donor, taker = mixed[0:amount // 2 * 2:2], mixed[1:amount // 2 * 2:2]
    room = jnp.minimum(sizes[donor] - 1, most - sizes[taker]) // 2
    room = jnp.where((donor == order[0]) | (taker == order[0]) | (sizes[taker] == 0), 0, jnp.maximum(room, 0))
    passed = jax.random.randint(jax.random.fold_in(own, 4), (amount // 2,), 0, 1 << 20) % (room + 1)
    sizes = sizes.at[donor].add(-passed).at[taker].add(passed)
    labels = jnp.searchsorted(jnp.cumsum(sizes), jnp.arange(rows * top), side="right").astype(jnp.int32)
    listing = labels.reshape(top, rows).T
    listing = listing[jax.random.permutation(jax.random.fold_in(own, 1), rows)]
    rotation = jax.random.randint(jax.random.fold_in(own, 2), (rows, 1), 0, top)
    return jnp.take_along_axis(listing, (jnp.arange(top)[None, :] + rotation) % top, axis=1)


def portions_of(amount, total, limit, lean, full):
    weights = [(1 << 20) // math.isqrt(standing ** lean) + 1 for standing in range(1, amount + 1)]
    largest = limit if full else min(limit, max(-(-total // amount), total * weights[0] // sum(weights)))
    least = 1 if total - largest >= amount - 1 else 0
    counts, surplus = [largest] + [least] * (amount - 1), total - largest - least * (amount - 1)
    while surplus > 0:
        movable = [i for i in range(1, amount) if counts[i] < largest] or [i for i in range(1, amount) if counts[i] < limit]
        whole, remaining = sum([weights[i] for i in movable]), surplus
        for i in movable:
            more = min(limit - counts[i], max(1, remaining * weights[i] // whole), surplus)
            counts[i] = counts[i] + more
            surplus = surplus - more
    return np.array(counts)


def bell_draw(stream_key, shape, spread, bound, cuts=(), held_as=jnp.bfloat16):
    result = jax.random.normal(stream_key, shape, jnp.float32) * spread
    if len(cuts) > 0:
        result = shard_levels(stream_key, shape, cuts, -0.22, 0.18) * result
    return jnp.clip(result, min=-bound, max=bound).astype(held_as)


def setup_inputs(seed: int = 0) -> dict:
    seeds = jax.random.split(jax.random.key(seed), 7)
    tokens = bell_draw(seeds[0], (TOKENS, D), 1.0, 6.0, ((0, 32),))
    gate_values = jnp.clip(0.2 + 0.8 * jax.random.uniform(seeds[1], (TOKENS, 2), jnp.float32) ** shard_levels(seeds[1], (TOKENS, 2), ((0, 32),), -0.2, 0.2), 0.2, 1.0)
    expert_ids_keys = jax.random.split(jax.random.fold_in(seeds[2], 1), TOKENS // TOK_DEV)
    expert_ids_turns = jax.random.permutation(jax.random.fold_in(seeds[2], 3), TOKENS // TOK_DEV)
    expert_ids = jax.vmap(lambda own, number: assign_block(jax.random.fold_in(seeds[2], 2), own, number, TOK_DEV, E, 2, CAP, 2))(expert_ids_keys, expert_ids_turns).reshape((TOKENS, 2))
    cotangent = bell_draw(seeds[3], (TOKENS, D), 1.0, 6.0, ((0, 32),))
    weight_in = bell_draw(seeds[4], (E * FF, D), D ** -0.5, 0.1875, ((0, 8),))
    weight_out = bell_draw(seeds[5], (E * FF, D), FF ** -0.5, 0.1875, ((0, 8),))
    return {"tokens": tokens, "gate_values": gate_values, "expert_ids": expert_ids, "cotangent": cotangent, "weight_in": weight_in, "weight_out": weight_out}


gelu_scale = 0.7978845608028654
gelu_cubic = 0.044715


def gelu_value(values):
    inner_arg = gelu_scale * (values + gelu_cubic * values * values * values)
    return 0.5 * values * (1.0 + jnp.tanh(inner_arg))


def gelu_slope(values):
    inner_arg = gelu_scale * (values + gelu_cubic * values * values * values)
    tanh_val = jnp.tanh(inner_arg)
    return 0.5 * (1.0 + tanh_val) + 0.5 * values * (1.0 - tanh_val * tanh_val) * gelu_scale * (1.0 + 3.0 * gelu_cubic * values * values)


def slot_numbers(ids_block):
    flat_ids = ids_block.reshape(-1)
    onehot = (flat_ids[:, None] == jnp.arange(E, dtype=jnp.int32)[None, :]).astype(jnp.int32)
    before = jnp.cumsum(onehot, axis=0) - onehot
    return jnp.sum(before * onehot, axis=1).reshape(ids_block.shape).astype(jnp.int32)


def fill_block(target_block, token_block, gate_block, cot_block):
    flat_target = target_block.reshape(-1)
    token_of = jnp.repeat(jnp.arange(TOK_DEV, dtype=jnp.int32), 2)
    slot_token = jnp.zeros((E * CAP,), jnp.int32).at[flat_target].set(token_of)
    slot_used = jnp.zeros((E * CAP,), jnp.float32).at[flat_target].set(1.0)
    slot_gate = jnp.zeros((E * CAP,), jnp.float32).at[flat_target].set(gate_block.reshape(-1))
    x_rows = (token_block[slot_token].astype(jnp.float32) * slot_used[:, None]).astype(jnp.bfloat16)
    d_rows = (cot_block[slot_token].astype(jnp.float32) * slot_gate[:, None]).astype(jnp.bfloat16)
    return x_rows, d_rows


def reference(tokens, gate_values, expert_ids, cotangent, weight_in, weight_out):
    factor = (E / (2.0 * TOKENS)) ** 0.5
    rows_group = N_SEQ * CAP
    win_all = weight_in.reshape(E, FF, D).astype(jnp.float32)
    wout_all = weight_out.reshape(E, FF, D).astype(jnp.float32)
    win_blocks = win_all.reshape(E, BLOCKS, BLOCK_UNITS, D)
    wout_blocks = wout_all.reshape(E, BLOCKS, BLOCK_UNITS, D)

    def one_group(carry, group_data):
        tok_group, gate_group, ids_group, cot_group = group_data
        slot_of = jax.vmap(slot_numbers)(ids_group)
        target = ids_group * CAP + slot_of
        x_buf, d_buf = jax.vmap(fill_block)(target, tok_group, gate_group, cot_group)
        x_buf = x_buf.reshape(N_SEQ, E, CAP, D).transpose(1, 0, 2, 3).reshape(E, rows_group, D)
        d_buf = d_buf.reshape(N_SEQ, E, CAP, D).transpose(1, 0, 2, 3).reshape(E, rows_group, D)
        x_float = x_buf.astype(jnp.float32)
        d_float = d_buf.astype(jnp.float32)
        hidden = jnp.einsum('erd,efd->erf', x_float, win_all)
        act = gelu_value(hidden).astype(jnp.bfloat16)
        act_float = act.astype(jnp.float32)
        part_out = jnp.einsum('erbh,ebhd->erbd', act_float.reshape(E, rows_group, BLOCKS, BLOCK_UNITS), wout_blocks).astype(jnp.bfloat16)
        back_hidden = jnp.einsum('erd,efd->erf', d_float, wout_all)
        dhid = (back_hidden * gelu_slope(hidden)).astype(jnp.bfloat16)
        dhid_float = dhid.astype(jnp.float32)
        part_in = jnp.einsum('erbh,ebhd->erbd', dhid_float.reshape(E, rows_group, BLOCKS, BLOCK_UNITS), win_blocks).astype(jnp.bfloat16)
        grad_out_group = (jnp.einsum('erd,erf->edf', d_float, act_float) * factor).astype(jnp.bfloat16)
        grad_in_group = (jnp.einsum('erd,erf->edf', x_float, dhid_float) * factor).astype(jnp.bfloat16)
        seq_index = jnp.arange(N_SEQ, dtype=jnp.int32)[:, None, None]
        rows_at = seq_index * CAP + slot_of
        expert_out = jnp.sum(part_out[ids_group, rows_at].astype(jnp.float32), axis=3)
        layer_part = jnp.sum(gate_group[..., None] * expert_out, axis=2).astype(jnp.bfloat16)
        gate_part = jnp.sum(cot_group.astype(jnp.float32)[:, :, None, :] * expert_out, axis=3)
        input_part = jnp.sum(part_in[ids_group, rows_at].astype(jnp.float32), axis=(2, 3)).astype(jnp.bfloat16)
        new_carry = (carry[0] + grad_in_group.astype(jnp.float32), carry[1] + grad_out_group.astype(jnp.float32))
        return new_carry, (layer_part, gate_part, input_part)

    group_data = (tokens.reshape(N_DP, N_SEQ, TOK_DEV, D), gate_values.reshape(N_DP, N_SEQ, TOK_DEV, 2),
                  expert_ids.reshape(N_DP, N_SEQ, TOK_DEV, 2), cotangent.reshape(N_DP, N_SEQ, TOK_DEV, D))
    start_carry = (jnp.zeros((E, D, FF), jnp.float32), jnp.zeros((E, D, FF), jnp.float32))
    final_carry, stacked = lax.scan(one_group, start_carry, group_data)
    layer_out = stacked[0].reshape(TOKENS, D)
    gate_grad = stacked[1].reshape(TOKENS, 2)
    input_grad = stacked[2].reshape(TOKENS, D)
    weight_in_grad = final_carry[0].transpose(1, 0, 2).reshape(D, E * FF)
    weight_out_grad = final_carry[1].transpose(1, 0, 2).reshape(D, E * FF)
    return layer_out, gate_grad, input_grad, weight_in_grad, weight_out_grad
```

```python
import functools

import jax
import jax.numpy as jnp
import numpy as np
from jax import lax
from jax.experimental import pallas as pl
from jax.experimental.pallas import tpu as pltpu
from jax.sharding import PartitionSpec as P

E = 32
FF = 1024
CAP = 9

BF16 = jnp.bfloat16
F32 = jnp.float32
VMEM_BYTES = 50 * 1024 * 1024

gelu_scale = 0.7978845608028654
gelu_cubic = 0.044715


def gelu_value(values):
    inner_arg = gelu_scale * (values + gelu_cubic * values * values * values)
    return 0.5 * values * (1.0 + jnp.tanh(inner_arg))


def gelu_slope(values):
    inner_arg = gelu_scale * (values + gelu_cubic * values * values * values)
    tanh_val = jnp.tanh(inner_arg)
    return 0.5 * (1.0 + tanh_val) + 0.5 * values * (1.0 - tanh_val * tanh_val) * gelu_scale * (
        1.0 + 3.0 * gelu_cubic * values * values
    )


def gelu_both(values):
    square = values * values
    tanh_val = jnp.tanh(gelu_scale * (values + gelu_cubic * square * values))
    half_up = 0.5 * (1.0 + tanh_val)
    slope = half_up + 0.5 * values * (1.0 - tanh_val * tanh_val) * gelu_scale * (
        1.0 + 3.0 * gelu_cubic * square
    )
    return values * half_up, slope


def iota(shape, dim):
    return lax.broadcasted_iota(jnp.int32, shape, dim)


def quotient(numbers, divisor):
    return jnp.floor((numbers.astype(F32) + 0.5) * (1.0 / divisor)).astype(jnp.int32)


def dot(a, b, dims):
    return lax.dot_general(a, b, ((dims[0], dims[1]), ((), ())), preferred_element_type=F32)


def ones_where(mask):
    return jnp.where(mask, 1.0, 0.0).astype(BF16)


def slab_slot(numbers, slots):
    slab = quotient(numbers, 2 * slots)
    rest = numbers - slab * (2 * slots)
    right = (rest >= slots).astype(jnp.int32)
    return slab * slots + rest - right * slots, right


def dispatch_kernel(slots, ids_ref, gate_ref, tok_ref, cot_ref, x_ref, d_ref, target_ref):
    count = tok_ref.shape[0]
    half = tok_ref.shape[1] // 2
    rows = x_ref.shape[0]
    ids = ids_ref[...]
    first, second = ids[0:1, :], ids[1:2, :]
    expert = iota((E, count), 0)
    hot_first, hot_second = expert == first, expert == second
    earlier = ones_where(iota((count, count), 0) < iota((count, count), 1))
    before = dot(ones_where(hot_first | hot_second), earlier, ((1,), (0,)))
    slot_first = jnp.sum(jnp.where(hot_first, before, 0.0), axis=0, keepdims=True)
    slot_second = jnp.sum(jnp.where(hot_second, before, 0.0), axis=0, keepdims=True)
    target_first = first * CAP + slot_first.astype(jnp.int32)
    target_second = second * CAP + slot_second.astype(jnp.int32)
    target_ref[0:1, :] = target_first
    target_ref[1:2, :] = target_second
    slot, right = slab_slot(iota((rows, 1), 0), slots)
    is_first, is_second = slot == target_first, slot == target_second
    pick = ones_where(is_first | is_second)
    is_right = right == 1
    rows_x = dot(pick, tok_ref[...], ((1,), (0,)))
    x_ref[...] = jnp.where(is_right, rows_x[:, half:], rows_x[:, :half]).astype(BF16)
    gates = gate_ref[...]
    gate = jnp.sum(
        jnp.where(is_first, gates[0:1, :], 0.0) + jnp.where(is_second, gates[1:2, :], 0.0),
        axis=1,
        keepdims=True,
    )
    rows_d = dot(pick, cot_ref[...], ((1,), (0,)))
    d_ref[...] = (jnp.where(is_right, rows_d[:, half:], rows_d[:, :half]) * gate).astype(BF16)


def group_rows(slab_ref, slots, held, sources):
    per_expert = sources * CAP
    number = iota((held * per_expert, 1), 0)
    expert = quotient(number, per_expert)
    rest = number - expert * per_expert
    source = quotient(rest, CAP)
    row = source * (2 * slots) + expert * CAP + rest - source * CAP
    at = iota((held * per_expert, 2 * slots * sources), 1)
    slabs = slab_ref[...]
    return [dot(ones_where(at == row + side * slots), slabs, ((1,), (0,))) for side in (0, 1)]


def slab_rows(rows, slots, held, sources):
    per_expert = sources * CAP
    half = rows.shape[1] // 2
    number = iota((2 * slots * sources, 1), 0)
    source = quotient(number, 2 * slots)
    rest = number - source * (2 * slots)
    is_right = rest >= slots
    rest = jnp.where(is_right, rest - slots, rest)
    expert = quotient(rest, CAP)
    row = expert * per_expert + source * CAP + rest - expert * CAP
    at = iota((2 * slots * sources, held * per_expert), 1)
    out = dot(ones_where(at == row), rows, ((1,), (0,)))
    return jnp.where(is_right, out[:, half:], out[:, :half])


def expert_kernel(
    slots, held, sources, forward, *refs
):
    if forward:
        slab_ref, up_ref, down_ref, out_ref, slope_ref, rows_ref, part_ref = refs
    else:
        slab_ref, slope_ref, up_ref, down_ref, out_ref, rows_ref, part_ref = refs
    step = pl.program_id(0)
    per_expert = sources * CAP
    half = slab_ref.shape[1]

    @pl.when(step == 0)
    def _():
        left, right = group_rows(slab_ref, slots, held, sources)
        for k in range(held):
            span = slice(k * per_expert, (k + 1) * per_expert)
            rows_ref[k, :, :half] = left[span].astype(BF16)
            rows_ref[k, :, half:] = right[span].astype(BF16)

    hidden = dot(rows_ref[step], up_ref[...], ((1,), (1,)))
    if forward:
        act, slope = gelu_both(hidden)
        slope_ref[0] = slope
    else:
        act = hidden * slope_ref[0]
    part = dot(act.astype(BF16), down_ref[...], ((1,), (0,)))
    part_ref[pl.ds(pl.multiple_of(step * per_expert, 8), per_expert), :] = part

    @pl.when(step == held - 1)
    def _():
        out_ref[...] = slab_rows(part_ref[...].astype(BF16), slots, held, sources).astype(BF16)


def hidden_kernel(slots, held, sources, groups, *refs):
    slab_refs, (column_ref, up_ref, act_ref, slope_ref, own_ref, rows_ref) = refs[:groups], refs[groups:]
    step = pl.program_id(0)
    half = slab_refs[0].shape[1]
    fill_rows(slab_refs, rows_ref, step, slots, held, sources)
    hidden = dot(rows_ref[step], up_ref[...], ((1,), (1,)))
    act, slope = gelu_both(hidden)
    act_ref[0] = act.astype(BF16)
    slope_ref[0] = slope.astype(BF16)
    wide = own_ref.shape[2]
    own_ref[0] = rows_ref[step, :, pl.ds(pl.multiple_of(column_ref[0], 128), wide)]


def fill_rows(slab_refs, rows_ref, step, slots, held, sources):
    per_expert = sources * CAP
    half = slab_refs[0].shape[1]

    @pl.when(step == 0)
    def _():
        grouped = [group_rows(ref, slots, held, sources) for ref in slab_refs]
        for side in (0, 1):
            for k in range(held):
                span = slice(k * per_expert, (k + 1) * per_expert)
                joined = jnp.concatenate([parts[side][span] for parts in grouped], axis=0)
                rows_ref[k, :, side * half : (side + 1) * half] = joined.astype(BF16)


def gradient_kernel(slots, held, sources, groups, factor, *refs):
    slab_refs = refs[:groups]
    column_ref, up_ref, act_ref, slope_ref, own_ref, grad_in_ref, grad_out_ref, rows_ref = refs[groups:]
    step = pl.program_id(0)
    fill_rows(slab_refs, rows_ref, step, slots, held, sources)
    back = dot(rows_ref[step], up_ref[...], ((1,), (1,)))
    dhid = (back * slope_ref[0].astype(F32)).astype(BF16)
    wide = own_ref.shape[2]
    own_d = rows_ref[step, :, pl.ds(pl.multiple_of(column_ref[0], 128), wide)]
    grad_in_ref[...] = dot(own_ref[0], dhid, ((0,), (0,))) * factor
    grad_out_ref[...] = dot(own_d, act_ref[0], ((0,), (0,))) * factor


def as_column(row):
    count = row.shape[1]
    same = iota((count, count), 0) == iota((count, count), 1)
    return jnp.sum(jnp.where(same, row, 0.0), axis=1, keepdims=True)


def as_row(column):
    count = column.shape[0]
    same = iota((count, count), 0) == iota((count, count), 1)
    return jnp.sum(jnp.where(same, column, 0.0), axis=0, keepdims=True)


def picked(target_ref, slots, rows):
    slot, right = slab_slot(iota((1, rows), 1), slots)
    columns = [as_column(target_ref[k : k + 1, :].astype(F32)).astype(jnp.int32) for k in (0, 1)]
    return [[(slot == column) & (right == side) for side in (0, 1)] for column in columns]


def output_kernel(slots, target_ref, gate_ref, cot_ref, back_ref, out_ref, gate_grad_ref):
    half = back_ref.shape[1]
    masks = picked(target_ref, slots, back_ref.shape[0])
    back = back_ref[...]
    gates = gate_ref[...]
    cot = cot_ref[...].astype(F32)
    layer, dots = [0.0, 0.0], []
    for k in (0, 1):
        gate = as_column(gates[k : k + 1, :])
        grad = 0.0
        for side in (0, 1):
            rows = dot(ones_where(masks[k][side]), back, ((1,), (0,)))
            layer[side] = layer[side] + gate * rows
            part = cot[:, side * half : (side + 1) * half] * rows
            grad = grad + jnp.sum(part, axis=1, keepdims=True)
        dots.append(as_row(grad))
    for side in (0, 1):
        out_ref[:, side * half : (side + 1) * half] = layer[side].astype(BF16)
    gate_grad_ref[...] = jnp.concatenate(dots, axis=0)


def input_kernel(slots, target_ref, back_ref, out_ref):
    half = back_ref.shape[1]
    masks = picked(target_ref, slots, back_ref.shape[0])
    back = back_ref[...]
    for side in (0, 1):
        pick = ones_where(masks[0][side] | masks[1][side])
        out_ref[:, side * half : (side + 1) * half] = dot(pick, back, ((1,), (0,))).astype(BF16)


def params():
    return pltpu.CompilerParams(vmem_limit_bytes=VMEM_BYTES)


def cost(flops, bytes_accessed):
    return pl.CostEstimate(flops=int(flops), bytes_accessed=int(bytes_accessed), transcendentals=0)


def local_rows(tokens, gate_values, expert_ids, cotangent, weight_in, weight_out):
    sources = lax.axis_size("seq")
    groups = lax.axis_size("dp")
    count, width = tokens.shape
    half = width // 2
    held = weight_in.shape[0] // FF
    slots = held * CAP
    per_expert = sources * CAP
    stacked = sources * 2 * slots
    factor = (E / (2.0 * count * sources * groups)) ** 0.5
    slab = jax.ShapeDtypeStruct((stacked, half), BF16)
    vmem = pl.BlockSpec(memory_space=pltpu.VMEM)

    def whole(shape):
        return pl.BlockSpec(shape, lambda k: (0,) * len(shape))

    def by_expert(shape):
        return pl.BlockSpec((1, *shape), lambda k: (k, 0, 0))

    weights = pl.BlockSpec((FF, width), lambda k: (k, 0))
    ids_rows, gate_rows = expert_ids.T, gate_values.T
    send_x, send_d, target = pl.pallas_call(
        functools.partial(dispatch_kernel, slots),
        out_shape=(slab, slab, jax.ShapeDtypeStruct((2, count), jnp.int32)),
        in_specs=[vmem] * 4,
        out_specs=(vmem,) * 3,
        compiler_params=params(),
        name="dispatch",
    )(ids_rows, gate_rows, tokens, cotangent)

    def exchange(stack):
        cut = stack.reshape(sources, 2 * slots, half)
        return lax.all_to_all(cut, "seq", split_axis=0, concat_axis=0, tiled=True).reshape(stacked, half)

    def from_peers(stack):
        got = [stack]
        bit = groups // 2
        while bit:
            pairs = [(i, i ^ bit) for i in range(groups)]
            got = got + [lax.ppermute(one, "dp", pairs) for one in got]
            bit = bit // 2
        return got

    product = 2 * held * per_expert * FF * width
    weight_bytes = 2 * weight_in.size

    got_x = exchange(send_x)
    got_d = exchange(send_d)
    all_x = from_peers(got_x)

    send_out, slope = pl.pallas_call(
        functools.partial(expert_kernel, slots, held, sources, True),
        grid=(held,),
        out_shape=(slab, jax.ShapeDtypeStruct((held, per_expert, FF), F32)),
        in_specs=[whole((stacked, half)), weights, weights],
        out_specs=(whole((stacked, half)), by_expert((per_expert, FF))),
        scratch_shapes=[
            pltpu.VMEM((held, per_expert, width), BF16),
            pltpu.VMEM((held * per_expert, width), F32),
        ],
        compiler_params=params(),
        cost_estimate=cost(2 * product, 2 * weight_bytes),
        name="expert_forward",
    )(got_x, weight_in, weight_out)
    got_out = exchange(send_out)
    all_d = from_peers(got_d)
    send_in = pl.pallas_call(
        functools.partial(expert_kernel, slots, held, sources, False),
        grid=(held,),
        out_shape=slab,
        in_specs=[whole((stacked, half)), by_expert((per_expert, FF)), weights, weights],
        out_specs=whole((stacked, half)),
        scratch_shapes=[
            pltpu.VMEM((held, per_expert, width), BF16),
            pltpu.VMEM((held * per_expert, width), F32),
        ],
        compiler_params=params(),
        cost_estimate=cost(2 * product, 2 * weight_bytes),
        name="expert_backward",
    )(got_d, slope, weight_out, weight_in)
    got_in = exchange(send_in)

    share = width // groups
    column = (lax.axis_index("dp") * share).astype(jnp.int32).reshape(1)
    scalar = pl.BlockSpec(memory_space=pltpu.SMEM)
    group_rows_count = groups * per_expert
    act, slope_all, own_x = pl.pallas_call(
        functools.partial(hidden_kernel, slots, held, sources, groups),
        grid=(held,),
        out_shape=(
            jax.ShapeDtypeStruct((held, group_rows_count, FF), BF16),
            jax.ShapeDtypeStruct((held, group_rows_count, FF), BF16),
            jax.ShapeDtypeStruct((held, group_rows_count, share), BF16),
        ),
        in_specs=[whole((stacked, half))] * groups + [scalar, weights],
        out_specs=(
            by_expert((group_rows_count, FF)),
            by_expert((group_rows_count, FF)),
            by_expert((group_rows_count, share)),
        ),
        scratch_shapes=[pltpu.VMEM((held, group_rows_count, width), BF16)],
        compiler_params=params(),
        cost_estimate=cost(groups * product, 2 * weight_bytes),
        name="hidden_all",
    )(*all_x, column, weight_in)
    gradient = jax.ShapeDtypeStruct((share, held * FF), F32)
    gradient_spec = pl.BlockSpec((share, FF), lambda k: (0, k))
    weight_in_grad, weight_out_grad = pl.pallas_call(
        functools.partial(gradient_kernel, slots, held, sources, groups, factor),
        grid=(held,),
        out_shape=(gradient, gradient),
        in_specs=[whole((stacked, half))] * groups
        + [
            scalar,
            weights,
            by_expert((group_rows_count, FF)),
            by_expert((group_rows_count, FF)),
            by_expert((group_rows_count, share)),
        ],
        out_specs=(gradient_spec, gradient_spec),
        scratch_shapes=[pltpu.VMEM((held, group_rows_count, width), BF16)],
        compiler_params=params(),
        cost_estimate=cost((groups + 2) * product, 4 * weight_bytes),
        name="gradients",
    )(*all_d, column, weight_out, act, slope_all, own_x)

    layer_out, gate_grad = pl.pallas_call(
        functools.partial(output_kernel, slots),
        out_shape=(
            jax.ShapeDtypeStruct((count, width), BF16),
            jax.ShapeDtypeStruct((2, count), F32),
        ),
        in_specs=[vmem] * 4,
        out_specs=(vmem, vmem),
        compiler_params=params(),
        name="combine_output",
    )(target, gate_rows, cotangent, got_out)
    input_grad = pl.pallas_call(
        functools.partial(input_kernel, slots),
        out_shape=jax.ShapeDtypeStruct((count, width), BF16),
        in_specs=[vmem] * 2,
        out_specs=vmem,
        compiler_params=params(),
        name="combine_input",
    )(target, got_in)
    return layer_out, gate_grad.T, input_grad, weight_in_grad, weight_out_grad


def slot_numbers(ids_block):
    flat_ids = ids_block.reshape(-1)
    onehot = (flat_ids[:, None] == jnp.arange(E, dtype=jnp.int32)[None, :]).astype(jnp.int32)
    before = jnp.cumsum(onehot, axis=0) - onehot
    return jnp.sum(before * onehot, axis=1).reshape(ids_block.shape)


def local_sums(tokens, gate_values, expert_ids, cotangent, weight_in, weight_out):
    seq_count = lax.axis_size("seq")
    group_count = lax.axis_size("dp")
    own_units = weight_in.shape[0]
    block_units = min(FF, own_units)
    held_experts = own_units // block_units
    block_count = FF // block_units
    tok_count = tokens.shape[0]
    model_width = tokens.shape[1]
    factor = (E / (2.0 * tok_count * seq_count * group_count)) ** 0.5
    row_total = seq_count * CAP
    slot_of = slot_numbers(expert_ids)
    flat_target = (expert_ids * CAP + slot_of).reshape(-1)
    token_of = jnp.repeat(jnp.arange(tok_count, dtype=jnp.int32), 2)
    slot_token = jnp.zeros((E * CAP,), jnp.int32).at[flat_target].set(token_of)
    slot_used = jnp.zeros((E * CAP,), jnp.float32).at[flat_target].set(1.0)
    slot_gate = jnp.zeros((E * CAP,), jnp.float32).at[flat_target].set(gate_values.reshape(-1))
    column = np.arange(seq_count * held_experts * CAP)
    owner_of = column // (held_experts * CAP)
    local_of = column // CAP % held_experts
    expert_of = (owner_of * own_units + local_of * block_units) // FF
    code_table = jnp.asarray(expert_of * CAP + column % CAP, dtype=jnp.int32)
    col_token = slot_token[code_table]
    col_used = slot_used[code_table]
    col_gate = slot_gate[code_table]
    send_shape = (seq_count, held_experts * CAP, model_width)
    send_x = (
        (tokens[col_token].astype(jnp.float32) * col_used[:, None])
        .astype(jnp.bfloat16)
        .reshape(send_shape)
    )
    send_d = (
        (cotangent[col_token].astype(jnp.float32) * col_gate[:, None])
        .astype(jnp.bfloat16)
        .reshape(send_shape)
    )
    win_local = weight_in.reshape(held_experts, block_units, model_width)
    wout_local = weight_out.reshape(held_experts, block_units, model_width)

    def to_rows(arrived):
        grouped = arrived.reshape(seq_count, held_experts, CAP, model_width)
        return jnp.transpose(grouped, (1, 0, 2, 3)).reshape(held_experts, row_total, model_width)

    def from_rows(results):
        grouped = results.reshape(held_experts, seq_count, CAP, model_width)
        return jnp.transpose(grouped, (1, 0, 2, 3)).reshape(send_shape)

    rows_x = to_rows(lax.all_to_all(send_x, "seq", split_axis=0, concat_axis=0, tiled=True))
    hidden = jnp.einsum("krd,kfd->krf", rows_x, win_local, preferred_element_type=jnp.float32)
    act = gelu_value(hidden).astype(jnp.bfloat16)
    part_out = jnp.einsum(
        "krf,kfd->krd", act, wout_local, preferred_element_type=jnp.float32
    ).astype(jnp.bfloat16)
    back_out = lax.all_to_all(from_rows(part_out), "seq", split_axis=0, concat_axis=0, tiled=True)
    rows_d = to_rows(lax.all_to_all(send_d, "seq", split_axis=0, concat_axis=0, tiled=True))
    back_hidden = jnp.einsum("krd,kfd->krf", rows_d, wout_local, preferred_element_type=jnp.float32)
    dhid = (back_hidden * gelu_slope(hidden)).astype(jnp.bfloat16)
    part_in = jnp.einsum(
        "krf,kfd->krd", dhid, win_local, preferred_element_type=jnp.float32
    ).astype(jnp.bfloat16)
    back_in = lax.all_to_all(from_rows(part_in), "seq", split_axis=0, concat_axis=0, tiled=True)

    def collect(returned):
        flat_rows = returned.reshape(-1, model_width)
        summed = jnp.zeros((tok_count, 2, model_width), jnp.float32)
        for block_index in range(block_count):
            unit_start = expert_ids * FF + block_index * block_units
            row_at = (
                unit_start // own_units * (held_experts * CAP)
                + unit_start % own_units // block_units * CAP
                + slot_of
            )
            summed = summed + flat_rows[row_at].astype(jnp.float32)
        return summed

    expert_out = collect(back_out)
    layer_out = jnp.sum(gate_values[:, :, None] * expert_out, axis=1).astype(jnp.bfloat16)
    gate_grad = jnp.sum(cotangent.astype(jnp.float32)[:, None, :] * expert_out, axis=2)
    input_grad = jnp.sum(collect(back_in), axis=1).astype(jnp.bfloat16)
    x_columns = jnp.transpose(rows_x, (2, 0, 1))
    d_columns = jnp.transpose(rows_d, (2, 0, 1))
    grad_in_part = (
        jnp.einsum("dkr,krf->dkf", x_columns, dhid, preferred_element_type=jnp.float32).reshape(
            model_width, own_units
        )
        * factor
    )
    grad_out_part = (
        jnp.einsum("dkr,krf->dkf", d_columns, act, preferred_element_type=jnp.float32).reshape(
            model_width, own_units
        )
        * factor
    )
    summed_grads = lax.psum_scatter(
        jnp.concatenate([grad_in_part, grad_out_part], axis=1).astype(jnp.bfloat16),
        "dp",
        scatter_dimension=0,
        tiled=True,
    ).astype(jnp.float32)
    weight_in_grad = summed_grads[:, :own_units]
    weight_out_grad = summed_grads[:, own_units:]
    return (layer_out, gate_grad, input_grad, weight_in_grad, weight_out_grad)


def local(tokens, gate_values, expert_ids, cotangent, weight_in, weight_out):
    units = weight_in.shape[0]
    row_values = lax.axis_size("seq") * max(units // FF, 1) * CAP * lax.axis_size("dp")
    if units % FF == 0 and row_values < units:
        plan = local_rows
    else:
        plan = local_sums
    return plan(tokens, gate_values, expert_ids, cotangent, weight_in, weight_out)


def solution(mesh):
    in_specs = (
        P(("dp", "seq"), None),
        P(("dp", "seq"), None),
        P(("dp", "seq"), None),
        P(("dp", "seq"), None),
        P("seq", None),
        P("seq", None),
    )
    out_specs = (
        P(("dp", "seq"), None),
        P(("dp", "seq"), None),
        P(("dp", "seq"), None),
        P("dp", "seq"),
        P("dp", "seq"),
    )
    return jax.shard_map(local, mesh=mesh, in_specs=in_specs, out_specs=out_specs, check_vma=False)
```

```python
import functools

import jax
import jax.numpy as jnp
import numpy as np
from jax import lax
from jax.experimental import pallas as pl
from jax.experimental.pallas import tpu as pltpu
from jax.sharding import PartitionSpec as P

E = 32
FF = 1024
CAP = 9

BF16 = jnp.bfloat16
F32 = jnp.float32

gelu_scale = 0.7978845608028654
gelu_cubic = 0.044715


def gelu_value(values):
    inner_arg = gelu_scale * (values + gelu_cubic * values * values * values)
    return 0.5 * values * (1.0 + jnp.tanh(inner_arg))


def gelu_slope(values):
    inner_arg = gelu_scale * (values + gelu_cubic * values * values * values)
    tanh_val = jnp.tanh(inner_arg)
    return 0.5 * (1.0 + tanh_val) + 0.5 * values * (1.0 - tanh_val * tanh_val) * gelu_scale * (
        1.0 + 3.0 * gelu_cubic * values * values
    )


def gelu_both(values):
    square = values * values
    tanh_val = jnp.tanh(gelu_scale * (values + gelu_cubic * square * values))
    half_up = 0.5 * (1.0 + tanh_val)
    slope = half_up + 0.5 * values * (1.0 - tanh_val * tanh_val) * gelu_scale * (
        1.0 + 3.0 * gelu_cubic * square
    )
    return values * half_up, slope


def iota(shape, dim):
    return lax.broadcasted_iota(jnp.int32, shape, dim)


def quotient(numbers, divisor):
    return jnp.floor((numbers.astype(F32) + 0.5) * (1.0 / divisor)).astype(jnp.int32)


def dot(a, b, dims):
    return lax.dot_general(a, b, ((dims[0], dims[1]), ((), ())), preferred_element_type=F32)


def ones_where(mask):
    return jnp.where(mask, 1.0, 0.0).astype(BF16)


def slab_slot(numbers, slots):
    slab = quotient(numbers, 2 * slots)
    rest = numbers - slab * (2 * slots)
    right = (rest >= slots).astype(jnp.int32)
    return slab * slots + rest - right * slots, right


def dispatch_kernel(
    slots, ids_hbm, gate_hbm, tok_hbm, cot_hbm, x_ref, d_ref, target_ref, ids_ref, gate_ref, tok_ref, cot_ref, sems
):
    copies = [
        pltpu.make_async_copy(source, here, sems.at[i])
        for i, (source, here) in enumerate(
            [(ids_hbm, ids_ref), (tok_hbm, tok_ref), (gate_hbm, gate_ref), (cot_hbm, cot_ref)]
        )
    ]
    for copy in copies:
        copy.start()
    count = tok_ref.shape[0]
    half = tok_ref.shape[1] // 2
    rows = x_ref.shape[0]
    copies[0].wait()
    ids = ids_ref[...]
    first, second = ids[0:1, :], ids[1:2, :]
    expert = iota((E, count), 0)
    hot_first, hot_second = expert == first, expert == second
    earlier = ones_where(iota((count, count), 0) < iota((count, count), 1))
    before = dot(ones_where(hot_first | hot_second), earlier, ((1,), (0,)))
    slot_first = jnp.sum(jnp.where(hot_first, before, 0.0), axis=0, keepdims=True)
    slot_second = jnp.sum(jnp.where(hot_second, before, 0.0), axis=0, keepdims=True)
    target_first = first * CAP + slot_first.astype(jnp.int32)
    target_second = second * CAP + slot_second.astype(jnp.int32)
    target_ref[0:1, :] = target_first
    target_ref[1:2, :] = target_second
    slot, right = slab_slot(iota((rows, 1), 0), slots)
    is_first, is_second = slot == target_first, slot == target_second
    pick = ones_where(is_first | is_second)
    is_right = right == 1
    copies[1].wait()
    rows_x = dot(pick, tok_ref[...], ((1,), (0,)))
    x_ref[...] = jnp.where(is_right, rows_x[:, half:], rows_x[:, :half]).astype(BF16)
    copies[2].wait()
    gates = gate_ref[...]
    gate = jnp.sum(
        jnp.where(is_first, gates[0:1, :], 0.0) + jnp.where(is_second, gates[1:2, :], 0.0),
        axis=1,
        keepdims=True,
    )
    copies[3].wait()
    rows_d = dot(pick, cot_ref[...], ((1,), (0,)))
    d_ref[...] = (jnp.where(is_right, rows_d[:, half:], rows_d[:, :half]) * gate).astype(BF16)


def regroup_kernel(slots, held, sources, slab_ref, rows_ref):
    per_expert = sources * CAP
    half = slab_ref.shape[1]
    number = iota((held * per_expert, 1), 0)
    expert = quotient(number, per_expert)
    rest = number - expert * per_expert
    source = quotient(rest, CAP)
    row = source * (2 * slots) + expert * CAP + rest - source * CAP
    at = iota((held * per_expert, 2 * slots * sources), 1)
    slabs = slab_ref[...]
    for side in (0, 1):
        rows = dot(ones_where(at == row + side * slots), slabs, ((1,), (0,)))
        for k in range(held):
            span = slice(k * per_expert, (k + 1) * per_expert)
            rows_ref[k, :, side * half : (side + 1) * half] = rows[span].astype(BF16)


def slab_rows(rows, slots, held, sources):
    per_expert = sources * CAP
    half = rows.shape[1] // 2
    number = iota((2 * slots * sources, 1), 0)
    source = quotient(number, 2 * slots)
    rest = number - source * (2 * slots)
    is_right = rest >= slots
    rest = jnp.where(is_right, rest - slots, rest)
    expert = quotient(rest, CAP)
    row = expert * per_expert + source * CAP + rest - expert * CAP
    at = iota((2 * slots * sources, held * per_expert), 1)
    out = dot(ones_where(at == row), rows, ((1,), (0,)))
    return jnp.where(is_right, out[:, half:], out[:, :half])


def weight_copies(up_hbm, down_hbm, up_ref, down_ref, sems):
    held = up_ref.shape[0]
    ups = [pltpu.make_async_copy(up_hbm.at[k], up_ref.at[k], sems.at[0, k]) for k in range(held)]
    downs = [pltpu.make_async_copy(down_hbm.at[k], down_ref.at[k], sems.at[1, k]) for k in range(held)]
    return ups, downs


def forward_kernel(
    slots, held, sources, rows_ref, up_hbm, down_hbm, out_ref, act_hbm, slope_hbm, up_ref, down_ref, act_ref, slope_ref, sems
):
    ups, downs = weight_copies(up_hbm, down_hbm, up_ref, down_ref, sems)
    for up, down in zip(ups, downs):
        up.start()
        down.start()
    parts, stores = [], []
    ups[0].wait()
    hidden = dot(rows_ref[0], up_ref[0], ((1,), (1,)))
    for k in range(held):
        now = hidden
        downs[k].wait()
        if k + 1 < held:
            ups[k + 1].wait()
            hidden = dot(rows_ref[k + 1], up_ref[k + 1], ((1,), (1,)))
        value, slope = gelu_both(now)
        act = value.astype(BF16)
        act_ref[k] = act
        slope_ref[k] = slope.astype(BF16)
        parts.append(dot(act, down_ref[k], ((1,), (0,))))
        for i, (here, there) in enumerate([(act_ref, act_hbm), (slope_ref, slope_hbm)]):
            stores.append(pltpu.make_async_copy(here.at[k], there.at[k], sems.at[2 + i, k]))
            stores[-1].start()
    rows = jnp.concatenate(parts, axis=0).astype(BF16)
    out_ref[...] = slab_rows(rows, slots, held, sources).astype(BF16)
    for store in stores:
        store.wait()


def backward_kernel(
    slots, held, sources, rows_ref, slope_hbm, up_hbm, down_hbm, out_ref, dhid_hbm, up_ref, down_ref, dhid_ref, slope_ref, sems
):
    ups, downs = weight_copies(up_hbm, down_hbm, up_ref, down_ref, sems)
    slopes = pltpu.make_async_copy(slope_hbm, slope_ref, sems.at[3, 0])
    for k in range(held):
        ups[k].start()
        if k == 0:
            slopes.start()
        downs[k].start()
    parts, stores = [], []
    ups[0].wait()
    back = dot(rows_ref[0], up_ref[0], ((1,), (1,)))
    slopes.wait()
    for k in range(held):
        now = back
        downs[k].wait()
        if k + 1 < held:
            ups[k + 1].wait()
            back = dot(rows_ref[k + 1], up_ref[k + 1], ((1,), (1,)))
        dhid = (now * slope_ref[k].astype(F32)).astype(BF16)
        dhid_ref[k] = dhid
        parts.append(dot(dhid, down_ref[k], ((1,), (0,))))
        stores.append(pltpu.make_async_copy(dhid_ref.at[k], dhid_hbm.at[k], sems.at[2, k]))
        stores[-1].start()
    rows = jnp.concatenate(parts, axis=0).astype(BF16)
    out_ref[...] = slab_rows(rows, slots, held, sources).astype(BF16)
    for store in stores:
        store.wait()


def gradient_kernel(peers, factor, share_ref, *refs):
    own_x_ref, own_d_ref, act_ref, dhid_ref, up_ref, down_ref = refs[:6]
    x_refs, d_refs = refs[6 : 6 + peers], refs[6 + peers : 6 + 2 * peers]
    grad_in_ref, grad_out_ref = refs[6 + 2 * peers :]
    wide = grad_in_ref.shape[0]
    share = pl.ds(pl.multiple_of(share_ref[0] * wide, 128), wide)
    rows_x = jnp.concatenate([ref[0] for ref in x_refs], axis=0)
    rows_d = jnp.concatenate([ref[0] for ref in d_refs], axis=0)
    hidden = dot(rows_x, up_ref[0], ((1,), (1,)))
    back = dot(rows_d, down_ref[0], ((1,), (1,)))
    value, slope = gelu_both(hidden)
    acts = jnp.concatenate([act_ref[0], value.astype(BF16)], axis=0)
    cut_d = jnp.concatenate([own_d_ref[0]] + [ref[0, :, share] for ref in d_refs], axis=0)
    grad_out_ref[...] = dot(cut_d, acts, ((0,), (0,))) * factor
    dhids = jnp.concatenate([dhid_ref[0], (back * slope).astype(BF16)], axis=0)
    cut_x = jnp.concatenate([own_x_ref[0]] + [ref[0, :, share] for ref in x_refs], axis=0)
    grad_in_ref[...] = dot(cut_x, dhids, ((0,), (0,))) * factor


def as_column(row):
    count = row.shape[1]
    same = iota((count, count), 0) == iota((count, count), 1)
    return jnp.sum(jnp.where(same, row, 0.0), axis=1, keepdims=True)


def as_row(column):
    count = column.shape[0]
    same = iota((count, count), 0) == iota((count, count), 1)
    return jnp.sum(jnp.where(same, column, 0.0), axis=0, keepdims=True)


def picked(target_ref, slots, rows):
    slot, right = slab_slot(iota((1, rows), 1), slots)
    columns = [as_column(target_ref[k : k + 1, :].astype(F32)).astype(jnp.int32) for k in (0, 1)]
    return [[(slot == column) & (right == side) for side in (0, 1)] for column in columns]


def output_kernel(slots, target_ref, gate_ref, cot_ref, back_ref, out_ref, gate_grad_ref):
    half = back_ref.shape[1]
    masks = picked(target_ref, slots, back_ref.shape[0])
    back = back_ref[...]
    gates = gate_ref[...]
    cot = cot_ref[...].astype(F32)
    layer, dots = [0.0, 0.0], []
    for k in (0, 1):
        gate = as_column(gates[k : k + 1, :])
        grad = 0.0
        for side in (0, 1):
            rows = dot(ones_where(masks[k][side]), back, ((1,), (0,)))
            layer[side] = layer[side] + gate * rows
            part = cot[:, side * half : (side + 1) * half] * rows
            grad = grad + jnp.sum(part, axis=1, keepdims=True)
        dots.append(as_row(grad))
    for side in (0, 1):
        out_ref[:, side * half : (side + 1) * half] = layer[side].astype(BF16)
    gate_grad_ref[...] = jnp.concatenate(dots, axis=0)


def input_kernel(slots, target_ref, back_ref, out_ref):
    half = back_ref.shape[1]
    masks = picked(target_ref, slots, back_ref.shape[0])
    back = back_ref[...]
    for side in (0, 1):
        pick = ones_where(masks[0][side] | masks[1][side])
        out_ref[:, side * half : (side + 1) * half] = dot(pick, back, ((1,), (0,))).astype(BF16)


def params(mib=58):
    return pltpu.CompilerParams(vmem_limit_bytes=mib * 1024 * 1024)


def cost(flops, bytes_accessed):
    return pl.CostEstimate(flops=int(flops), bytes_accessed=int(bytes_accessed), transcendentals=0)


def vmem_call(kernel, outs, args, name, estimate=None, mib=6):
    vmem = pl.BlockSpec(memory_space=pltpu.VMEM)
    return pl.pallas_call(
        kernel,
        out_shape=outs,
        in_specs=[vmem] * len(args),
        out_specs=jax.tree.map(lambda _: vmem, outs),
        compiler_params=params(mib),
        cost_estimate=estimate,
        name=name,
    )(*args)


def local_rows(tokens, gate_values, expert_ids, cotangent, weight_in, weight_out):
    sources = lax.axis_size("seq")
    groups = lax.axis_size("dp")
    peers = groups - 1
    count, width = tokens.shape
    half = width // 2
    held = weight_in.shape[0] // FF
    slots = held * CAP
    per_expert = sources * CAP
    stacked = sources * 2 * slots
    factor = (E / (2.0 * count * sources * groups)) ** 0.5
    slab = jax.ShapeDtypeStruct((stacked, half), BF16)
    rows_shape = jax.ShapeDtypeStruct((held, per_expert, width), BF16)
    units_shape = jax.ShapeDtypeStruct((held, per_expert, FF), BF16)
    product = 2 * held * per_expert * FF * width
    vmem = pl.BlockSpec(memory_space=pltpu.VMEM)

    hbm = pl.BlockSpec(memory_space=pltpu.HBM)
    sems = pltpu.SemaphoreType.DMA

    ids_rows, gate_rows = expert_ids.T, gate_values.T
    send_x, send_d, target = pl.pallas_call(
        functools.partial(dispatch_kernel, slots),
        out_shape=(slab, slab, jax.ShapeDtypeStruct((2, count), jnp.int32)),
        in_specs=[hbm] * 4,
        out_specs=(vmem,) * 3,
        scratch_shapes=[
            pltpu.VMEM((2, count), jnp.int32),
            pltpu.VMEM((2, count), F32),
            pltpu.VMEM((count, width), BF16),
            pltpu.VMEM((count, width), BF16),
            sems((4,)),
        ],
        compiler_params=params(),
        name="dispatch",
    )(ids_rows, gate_rows, tokens, cotangent)
    win = weight_in.reshape(held, FF, width)
    wout = weight_out.reshape(held, FF, width)

    def exchange(stack):
        cut = stack.reshape(sources, 2 * slots, half)
        return lax.all_to_all(cut, "seq", split_axis=0, concat_axis=0, tiled=True).reshape(stacked, half)

    def regroup(stack):
        return vmem_call(
            functools.partial(regroup_kernel, slots, held, sources),
            rows_shape,
            [stack],
            "regroup",
            cost(product, 4 * stacked * half),
        )

    def across(rows, bit):
        return lax.ppermute(rows, "dp", [(i, i ^ bit) for i in range(groups)])

    got_x = exchange(send_x)
    got_d = exchange(send_d)
    rows_x = regroup(got_x)
    peers_x = [rows_x]
    far = groups // 2
    first_x = across(rows_x, far)

    units = pltpu.VMEM((held, per_expert, FF), BF16)
    experts = pltpu.VMEM((held, FF, width), BF16)
    send_out, act, slope = pl.pallas_call(
        functools.partial(forward_kernel, slots, held, sources),
        out_shape=(slab, units_shape, units_shape),
        in_specs=[vmem, hbm, hbm],
        out_specs=(vmem, hbm, hbm),
        scratch_shapes=[experts, experts, units, units, sems((4, held))],
        compiler_params=params(),
        cost_estimate=cost(4 * product, 4 * weight_in.size),
        name="expert_forward",
    )(rows_x, win, wout)
    got_out = exchange(send_out)
    got_d, first_x = lax.optimization_barrier((got_d, first_x))
    rows_d = regroup(got_d)
    first_d = across(rows_d, far)

    def from_peers(rows, first):
        got, bit = [rows, first], far // 2
        while bit:
            got = got + [across(one, bit) for one in got]
            bit = bit // 2
        return got

    all_x = from_peers(rows_x, first_x)
    send_in, dhid = pl.pallas_call(
        functools.partial(backward_kernel, slots, held, sources),
        out_shape=(slab, units_shape),
        in_specs=[vmem, hbm, hbm, hbm],
        out_specs=(vmem, hbm),
        scratch_shapes=[experts, experts, units, units, sems((4, held))],
        compiler_params=params(),
        cost_estimate=cost(4 * product, 4 * weight_in.size),
        name="expert_backward",
    )(rows_d, slope, wout, win)
    send_in, *all_x = lax.optimization_barrier((send_in, *all_x))
    first_d, rows_d, dhid = lax.optimization_barrier((first_d, rows_d, dhid))
    got_in = exchange(send_in)
    all_d = from_peers(rows_d, first_d)

    share = width // groups
    index = lax.axis_index("dp").astype(jnp.int32).reshape(1)
    gradient = jax.ShapeDtypeStruct((share, held * FF), F32)
    parts = 2
    some = FF // parts
    gradient_spec = pl.BlockSpec((share, some), lambda k, f, index: (0, k * parts + f))
    cut = pl.BlockSpec((1, per_expert, share), lambda k, f, index: (k, 0, index[0]))
    full = pl.BlockSpec((1, per_expert, width), lambda k, f, index: (k, 0, 0))
    own = pl.BlockSpec((1, per_expert, some), lambda k, f, index: (k, 0, f))
    weights = pl.BlockSpec((1, some, width), lambda k, f, index: (k, f, 0))
    weight_in_grad, weight_out_grad = pl.pallas_call(
        functools.partial(gradient_kernel, peers, factor),
        out_shape=(gradient, gradient),
        grid_spec=pltpu.PrefetchScalarGridSpec(
            num_scalar_prefetch=1,
            grid=(held, parts),
            in_specs=[cut, cut, own, own, weights, weights] + [full] * (2 * peers),
            out_specs=(gradient_spec, gradient_spec),
        ),
        compiler_params=params(),
        cost_estimate=cost(12 * product, 8 * weight_in.size),
        name="gradients",
    )(index, rows_x, rows_d, act, dhid, win, wout, *all_x[1:], *all_d[1:])

    layer_out, gate_grad = vmem_call(
        functools.partial(output_kernel, slots),
        (jax.ShapeDtypeStruct((count, width), BF16), jax.ShapeDtypeStruct((2, count), F32)),
        [target, gate_rows, cotangent, got_out],
        "combine_output",
    )
    got_in, weight_in_grad = lax.optimization_barrier((got_in, weight_in_grad))
    input_grad = vmem_call(
        functools.partial(input_kernel, slots),
        jax.ShapeDtypeStruct((count, width), BF16),
        [target, got_in],
        "combine_input",
    )
    return layer_out, gate_grad.T, input_grad, weight_in_grad, weight_out_grad


def slot_numbers(ids_block):
    flat_ids = ids_block.reshape(-1)
    onehot = (flat_ids[:, None] == jnp.arange(E, dtype=jnp.int32)[None, :]).astype(jnp.int32)
    before = jnp.cumsum(onehot, axis=0) - onehot
    return jnp.sum(before * onehot, axis=1).reshape(ids_block.shape)


def local_sums(tokens, gate_values, expert_ids, cotangent, weight_in, weight_out):
    seq_count = lax.axis_size("seq")
    group_count = lax.axis_size("dp")
    own_units = weight_in.shape[0]
    block_units = min(FF, own_units)
    held_experts = own_units // block_units
    block_count = FF // block_units
    tok_count = tokens.shape[0]
    model_width = tokens.shape[1]
    factor = (E / (2.0 * tok_count * seq_count * group_count)) ** 0.5
    row_total = seq_count * CAP
    slot_of = slot_numbers(expert_ids)
    flat_target = (expert_ids * CAP + slot_of).reshape(-1)
    token_of = jnp.repeat(jnp.arange(tok_count, dtype=jnp.int32), 2)
    slot_token = jnp.zeros((E * CAP,), jnp.int32).at[flat_target].set(token_of)
    slot_used = jnp.zeros((E * CAP,), jnp.float32).at[flat_target].set(1.0)
    slot_gate = jnp.zeros((E * CAP,), jnp.float32).at[flat_target].set(gate_values.reshape(-1))
    column = np.arange(seq_count * held_experts * CAP)
    owner_of = column // (held_experts * CAP)
    local_of = column // CAP % held_experts
    expert_of = (owner_of * own_units + local_of * block_units) // FF
    code_table = jnp.asarray(expert_of * CAP + column % CAP, dtype=jnp.int32)
    col_token = slot_token[code_table]
    col_used = slot_used[code_table]
    col_gate = slot_gate[code_table]
    send_shape = (seq_count, held_experts * CAP, model_width)
    send_x = (
        (tokens[col_token].astype(jnp.float32) * col_used[:, None])
        .astype(jnp.bfloat16)
        .reshape(send_shape)
    )
    send_d = (
        (cotangent[col_token].astype(jnp.float32) * col_gate[:, None])
        .astype(jnp.bfloat16)
        .reshape(send_shape)
    )
    win_local = weight_in.reshape(held_experts, block_units, model_width)
    wout_local = weight_out.reshape(held_experts, block_units, model_width)

    def to_rows(arrived):
        grouped = arrived.reshape(seq_count, held_experts, CAP, model_width)
        return jnp.transpose(grouped, (1, 0, 2, 3)).reshape(held_experts, row_total, model_width)

    def from_rows(results):
        grouped = results.reshape(held_experts, seq_count, CAP, model_width)
        return jnp.transpose(grouped, (1, 0, 2, 3)).reshape(send_shape)

    rows_x = to_rows(lax.all_to_all(send_x, "seq", split_axis=0, concat_axis=0, tiled=True))
    hidden = jnp.einsum("krd,kfd->krf", rows_x, win_local, preferred_element_type=jnp.float32)
    act = gelu_value(hidden).astype(jnp.bfloat16)
    part_out = jnp.einsum(
        "krf,kfd->krd", act, wout_local, preferred_element_type=jnp.float32
    ).astype(jnp.bfloat16)
    back_out = lax.all_to_all(from_rows(part_out), "seq", split_axis=0, concat_axis=0, tiled=True)
    rows_d = to_rows(lax.all_to_all(send_d, "seq", split_axis=0, concat_axis=0, tiled=True))
    back_hidden = jnp.einsum("krd,kfd->krf", rows_d, wout_local, preferred_element_type=jnp.float32)
    dhid = (back_hidden * gelu_slope(hidden)).astype(jnp.bfloat16)
    part_in = jnp.einsum(
        "krf,kfd->krd", dhid, win_local, preferred_element_type=jnp.float32
    ).astype(jnp.bfloat16)
    back_in = lax.all_to_all(from_rows(part_in), "seq", split_axis=0, concat_axis=0, tiled=True)

    def collect(returned):
        flat_rows = returned.reshape(-1, model_width)
        summed = jnp.zeros((tok_count, 2, model_width), jnp.float32)
        for block_index in range(block_count):
            unit_start = expert_ids * FF + block_index * block_units
            row_at = (
                unit_start // own_units * (held_experts * CAP)
                + unit_start % own_units // block_units * CAP
                + slot_of
            )
            summed = summed + flat_rows[row_at].astype(jnp.float32)
        return summed

    expert_out = collect(back_out)
    layer_out = jnp.sum(gate_values[:, :, None] * expert_out, axis=1).astype(jnp.bfloat16)
    gate_grad = jnp.sum(cotangent.astype(jnp.float32)[:, None, :] * expert_out, axis=2)
    input_grad = jnp.sum(collect(back_in), axis=1).astype(jnp.bfloat16)
    x_columns = jnp.transpose(rows_x, (2, 0, 1))
    d_columns = jnp.transpose(rows_d, (2, 0, 1))
    grad_in_part = (
        jnp.einsum("dkr,krf->dkf", x_columns, dhid, preferred_element_type=jnp.float32).reshape(
            model_width, own_units
        )
        * factor
    )
    grad_out_part = (
        jnp.einsum("dkr,krf->dkf", d_columns, act, preferred_element_type=jnp.float32).reshape(
            model_width, own_units
        )
        * factor
    )
    summed_grads = lax.psum_scatter(
        jnp.concatenate([grad_in_part, grad_out_part], axis=1).astype(jnp.bfloat16),
        "dp",
        scatter_dimension=0,
        tiled=True,
    ).astype(jnp.float32)
    weight_in_grad = summed_grads[:, :own_units]
    weight_out_grad = summed_grads[:, own_units:]
    return (layer_out, gate_grad, input_grad, weight_in_grad, weight_out_grad)


def local(tokens, gate_values, expert_ids, cotangent, weight_in, weight_out):
    units = weight_in.shape[0]
    row_values = lax.axis_size("seq") * max(units // FF, 1) * CAP * lax.axis_size("dp")
    if units % FF == 0 and row_values < units:
        plan = local_rows
    else:
        plan = local_sums
    return plan(tokens, gate_values, expert_ids, cotangent, weight_in, weight_out)


def solution(mesh):
    in_specs = (
        P(("dp", "seq"), None),
        P(("dp", "seq"), None),
        P(("dp", "seq"), None),
        P(("dp", "seq"), None),
        P("seq", None),
        P("seq", None),
    )
    out_specs = (
        P(("dp", "seq"), None),
        P(("dp", "seq"), None),
        P(("dp", "seq"), None),
        P("dp", "seq"),
        P("dp", "seq"),
    )
    return jax.shard_map(local, mesh=mesh, in_specs=in_specs, out_specs=out_specs, check_vma=False)
```

```python
import functools

import jax
import jax.numpy as jnp
import numpy as np
from jax import lax
from jax.experimental import pallas as pl
from jax.experimental.pallas import tpu as pltpu
from jax.sharding import PartitionSpec as P

E = 32
FF = 1024
CAP = 9

BF16 = jnp.bfloat16
F32 = jnp.float32

gelu_scale = 0.7978845608028654
gelu_cubic = 0.044715


def gelu_value(values):
    inner_arg = gelu_scale * (values + gelu_cubic * values * values * values)
    return 0.5 * values * (1.0 + jnp.tanh(inner_arg))


def gelu_slope(values):
    inner_arg = gelu_scale * (values + gelu_cubic * values * values * values)
    tanh_val = jnp.tanh(inner_arg)
    return 0.5 * (1.0 + tanh_val) + 0.5 * values * (1.0 - tanh_val * tanh_val) * gelu_scale * (
        1.0 + 3.0 * gelu_cubic * values * values
    )


def gelu_both(values):
    square = values * values
    tanh_val = jnp.tanh(gelu_scale * (values + gelu_cubic * square * values))
    half_up = 0.5 * (1.0 + tanh_val)
    slope = half_up + 0.5 * values * (1.0 - tanh_val * tanh_val) * gelu_scale * (
        1.0 + 3.0 * gelu_cubic * square
    )
    return values * half_up, slope


def iota(shape, dim):
    return lax.broadcasted_iota(jnp.int32, shape, dim)


def quotient(numbers, divisor):
    return jnp.floor((numbers.astype(F32) + 0.5) * (1.0 / divisor)).astype(jnp.int32)


def dot(a, b, dims):
    return lax.dot_general(a, b, ((dims[0], dims[1]), ((), ())), preferred_element_type=F32)


def ones_where(mask):
    return jnp.where(mask, 1.0, 0.0).astype(BF16)


def slab_slot(numbers, slots):
    slab = quotient(numbers, 2 * slots)
    rest = numbers - slab * (2 * slots)
    right = rest >= slots
    return slab, jnp.where(right, rest - slots, rest), right


def here(axis):
    return lax.axis_index(axis).astype(jnp.int32)


def token_kernel(slots, sources, ids_hbm, tok_hbm, *refs):
    slab_refs, (target_ref, ids_ref, tok_ref, sems) = refs[:sources], refs[sources:]
    ids_copy = pltpu.make_async_copy(ids_hbm, ids_ref, sems.at[0])
    tok_copy = pltpu.make_async_copy(tok_hbm, tok_ref, sems.at[1])
    ids_copy.start()
    tok_copy.start()
    count = tok_ref.shape[0]
    half = tok_ref.shape[1] // 2
    expert = iota((E, count), 0)
    earlier = ones_where(iota((count, count), 0) < iota((count, count), 1))
    slab, slot, right = slab_slot(iota((sources * 2 * slots, 1), 0), slots)
    slot = (slab ^ here("seq")) * slots + slot
    ids_copy.wait()
    ids = ids_ref[...]
    first, second = ids[0:1, :], ids[1:2, :]
    hot_first, hot_second = expert == first, expert == second
    before = dot(ones_where(hot_first | hot_second), earlier, ((1,), (0,)))
    slot_first = jnp.sum(jnp.where(hot_first, before, 0.0), axis=0, keepdims=True)
    slot_second = jnp.sum(jnp.where(hot_second, before, 0.0), axis=0, keepdims=True)
    target_first = first * CAP + slot_first.astype(jnp.int32)
    target_second = second * CAP + slot_second.astype(jnp.int32)
    target_ref[0:1, :] = target_first
    target_ref[1:2, :] = target_second
    pick = ones_where((slot == target_first) | (slot == target_second))
    tok_copy.wait()
    rows = dot(pick, tok_ref[...], ((1,), (0,)))
    rows = jnp.where(right, rows[:, half:], rows[:, :half]).astype(BF16)
    for j, slab_ref in enumerate(slab_refs):
        slab_ref[...] = rows[j * 2 * slots : (j + 1) * 2 * slots]


def cotangent_kernel(slots, target_ref, gate_ref, cot_hbm, slab_ref, cot_ref, sem):
    copy = pltpu.make_async_copy(cot_hbm, cot_ref, sem)
    copy.start()
    half = cot_ref.shape[1] // 2
    slab, slot, right = slab_slot(iota((slab_ref.shape[0], 1), 0), slots)
    slot = slab * slots + slot
    is_first, is_second = slot == target_ref[0:1, :], slot == target_ref[1:2, :]
    gate = jnp.sum(
        jnp.where(is_first, gate_ref[0:1, :], 0.0) + jnp.where(is_second, gate_ref[1:2, :], 0.0),
        axis=1,
        keepdims=True,
    )
    copy.wait()
    rows = dot(ones_where(is_first | is_second), cot_ref[...], ((1,), (0,)))
    slab_ref[...] = (jnp.where(right, rows[:, half:], rows[:, :half]) * gate).astype(BF16)


def regroup_kernel(slots, held, sources, *refs):
    slab_refs, rows_ref = refs[:-1], refs[-1]
    per_expert = sources * CAP
    half = slab_refs[0].shape[1]
    number = iota((held * per_expert, 1), 0)
    expert = quotient(number, per_expert)
    rest = number - expert * per_expert
    source = quotient(rest, CAP)
    slab = source ^ here("seq") if len(slab_refs) > 1 else source
    row = slab * (2 * slots) + expert * CAP + rest - source * CAP
    at = iota((held * per_expert, 2 * slots * sources), 1)
    slabs = jnp.concatenate([ref[...] for ref in slab_refs], axis=0)
    for side in (0, 1):
        rows = dot(ones_where(at == row + side * slots), slabs, ((1,), (0,)))
        for k in range(held):
            span = slice(k * per_expert, (k + 1) * per_expert)
            rows_ref[k, :, side * half : (side + 1) * half] = rows[span].astype(BF16)


def slab_rows(parts, slots, held, sources):
    per_expert = sources * CAP
    rows = jnp.concatenate(parts, axis=0).astype(BF16)
    half = rows.shape[1] // 2
    source, slot, right = slab_slot(iota((2 * slots * sources, 1), 0), slots)
    expert = quotient(slot, CAP)
    row = expert * per_expert + source * CAP + slot - expert * CAP
    out = dot(ones_where(iota((2 * slots * sources, held * per_expert), 1) == row), rows, ((1,), (0,)))
    return jnp.where(right, out[:, half:], out[:, :half]).astype(BF16)


def weight_copies(up_hbm, down_hbm, up_ref, down_ref, sems):
    held = up_ref.shape[0]
    ups = [pltpu.make_async_copy(up_hbm.at[k], up_ref.at[k], sems.at[0, k]) for k in range(held)]
    downs = [pltpu.make_async_copy(down_hbm.at[k], down_ref.at[k], sems.at[1, k]) for k in range(held)]
    return ups, downs


def forward_kernel(
    slots, held, sources, rows_ref, up_hbm, down_hbm, out_ref, act_hbm, slope_hbm, up_ref, down_ref, act_ref, slope_ref, sems
):
    ups, downs = weight_copies(up_hbm, down_hbm, up_ref, down_ref, sems)
    for up, down in zip(ups, downs):
        up.start()
        down.start()
    parts, stores = [], []
    ups[0].wait()
    hidden = dot(rows_ref[0], up_ref[0], ((1,), (1,)))
    for k in range(held):
        now = hidden
        downs[k].wait()
        if k + 1 < held:
            ups[k + 1].wait()
            hidden = dot(rows_ref[k + 1], up_ref[k + 1], ((1,), (1,)))
        value, slope = gelu_both(now)
        act = value.astype(BF16)
        act_ref[k] = act
        slope_ref[k] = slope.astype(BF16)
        parts.append(dot(act, down_ref[k], ((1,), (0,))))
        for i, (here, there) in enumerate([(act_ref, act_hbm), (slope_ref, slope_hbm)]):
            stores.append(pltpu.make_async_copy(here.at[k], there.at[k], sems.at[2 + i, k]))
            stores[-1].start()
    out_ref[...] = slab_rows(parts, slots, held, sources)
    for store in stores:
        store.wait()


def backward_kernel(
    slots, held, sources, rows_ref, slope_hbm, up_hbm, down_hbm, out_ref, dhid_hbm, up_ref, down_ref, dhid_ref, slope_ref, sems
):
    ups, downs = weight_copies(up_hbm, down_hbm, up_ref, down_ref, sems)
    slopes = pltpu.make_async_copy(slope_hbm, slope_ref, sems.at[3, 0])
    for k in range(held):
        ups[k].start()
        if k == 0:
            slopes.start()
        downs[k].start()
    parts, stores = [], []
    ups[0].wait()
    back = dot(rows_ref[0], up_ref[0], ((1,), (1,)))
    slopes.wait()
    for k in range(held):
        now = back
        downs[k].wait()
        if k + 1 < held:
            ups[k + 1].wait()
            back = dot(rows_ref[k + 1], up_ref[k + 1], ((1,), (1,)))
        dhid = (now * slope_ref[k].astype(F32)).astype(BF16)
        dhid_ref[k] = dhid
        parts.append(dot(dhid, down_ref[k], ((1,), (0,))))
        stores.append(pltpu.make_async_copy(dhid_ref.at[k], dhid_hbm.at[k], sems.at[2, k]))
        stores[-1].start()
    out_ref[...] = slab_rows(parts, slots, held, sources)
    for store in stores:
        store.wait()


def gradient_kernel(peers, factor, share_ref, *refs):
    own_x_ref, own_d_ref, act_ref, dhid_ref, up_ref, down_ref = refs[:6]
    x_refs, d_refs = refs[6 : 6 + peers], refs[6 + peers : 6 + 2 * peers]
    grad_in_ref, grad_out_ref = refs[6 + 2 * peers :]
    wide = grad_in_ref.shape[0]
    share = pl.ds(pl.multiple_of(share_ref[0] * wide, 128), wide)
    rows_x = jnp.concatenate([ref[0] for ref in x_refs], axis=0)
    rows_d = jnp.concatenate([ref[0] for ref in d_refs], axis=0)
    hidden = dot(rows_x, up_ref[0], ((1,), (1,)))
    back = dot(rows_d, down_ref[0], ((1,), (1,)))
    value, slope = gelu_both(hidden)
    acts = jnp.concatenate([act_ref[0], value.astype(BF16)], axis=0)
    cut_d = jnp.concatenate([own_d_ref[0]] + [ref[0, :, share] for ref in d_refs], axis=0)
    grad_out_ref[...] = dot(cut_d, acts, ((0,), (0,))) * factor
    dhids = jnp.concatenate([dhid_ref[0], (back * slope).astype(BF16)], axis=0)
    cut_x = jnp.concatenate([own_x_ref[0]] + [ref[0, :, share] for ref in x_refs], axis=0)
    grad_in_ref[...] = dot(cut_x, dhids, ((0,), (0,))) * factor


def as_column(row):
    count = row.shape[1]
    same = iota((count, count), 0) == iota((count, count), 1)
    return jnp.sum(jnp.where(same, row, 0.0), axis=1, keepdims=True)


def as_row(column):
    count = column.shape[0]
    same = iota((count, count), 0) == iota((count, count), 1)
    return jnp.sum(jnp.where(same, column, 0.0), axis=0, keepdims=True)


def picked(target_ref, slots, rows):
    slab, slot, right = slab_slot(iota((1, rows), 1), slots)
    slot = slab * slots + slot
    columns = [as_column(target_ref[k : k + 1, :].astype(F32)).astype(jnp.int32) for k in (0, 1)]
    return [[(slot == column) & ~right, (slot == column) & right] for column in columns]


def output_kernel(slots, target_ref, gate_ref, cot_ref, back_ref, out_ref, gate_grad_ref):
    half = back_ref.shape[1]
    masks = picked(target_ref, slots, back_ref.shape[0])
    back = back_ref[...]
    gates = gate_ref[...]
    cot = cot_ref[...].astype(F32)
    layer, dots = [0.0, 0.0], []
    for k in (0, 1):
        gate = as_column(gates[k : k + 1, :])
        grad = 0.0
        for side in (0, 1):
            rows = dot(ones_where(masks[k][side]), back, ((1,), (0,)))
            layer[side] = layer[side] + gate * rows
            part = cot[:, side * half : (side + 1) * half] * rows
            grad = grad + jnp.sum(part, axis=1, keepdims=True)
        dots.append(as_row(grad))
    for side in (0, 1):
        out_ref[:, side * half : (side + 1) * half] = layer[side].astype(BF16)
    gate_grad_ref[...] = jnp.concatenate(dots, axis=0)


def input_kernel(slots, target_ref, back_ref, out_ref):
    half = back_ref.shape[1]
    masks = picked(target_ref, slots, back_ref.shape[0])
    back = back_ref[...]
    for side in (0, 1):
        pick = ones_where(masks[0][side] | masks[1][side])
        out_ref[:, side * half : (side + 1) * half] = dot(pick, back, ((1,), (0,))).astype(BF16)


def params(mib=58):
    return pltpu.CompilerParams(vmem_limit_bytes=mib * 1024 * 1024)


def cost(flops, bytes_accessed):
    return pl.CostEstimate(flops=int(flops), bytes_accessed=int(bytes_accessed), transcendentals=0)


def vmem_call(kernel, outs, args, name, estimate=None, mib=6):
    vmem = pl.BlockSpec(memory_space=pltpu.VMEM)
    return pl.pallas_call(
        kernel,
        out_shape=outs,
        in_specs=[vmem] * len(args),
        out_specs=jax.tree.map(lambda _: vmem, outs),
        compiler_params=params(mib),
        cost_estimate=estimate,
        name=name,
    )(*args)


def local_rows(tokens, gate_values, expert_ids, cotangent, weight_in, weight_out):
    sources = lax.axis_size("seq")
    groups = lax.axis_size("dp")
    peers = groups - 1
    count, width = tokens.shape
    half = width // 2
    held = weight_in.shape[0] // FF
    slots = held * CAP
    per_expert = sources * CAP
    stacked = sources * 2 * slots
    factor = (E / (2.0 * count * sources * groups)) ** 0.5
    slab = jax.ShapeDtypeStruct((stacked, half), BF16)
    rows_shape = jax.ShapeDtypeStruct((held, per_expert, width), BF16)
    units_shape = jax.ShapeDtypeStruct((held, per_expert, FF), BF16)
    peers_shape = jax.ShapeDtypeStruct((held, peers * per_expert, FF), BF16)
    product = 2 * held * per_expert * FF * width
    vmem = pl.BlockSpec(memory_space=pltpu.VMEM)

    hbm = pl.BlockSpec(memory_space=pltpu.HBM)
    sems = pltpu.SemaphoreType.DMA

    def by_expert(shape):
        return pl.BlockSpec((1, *shape), lambda k, *_: (k, 0, 0))

    ids_rows, gate_rows = expert_ids.T, gate_values.T
    piece = jax.ShapeDtypeStruct((2 * slots, half), BF16)
    *pieces, target = pl.pallas_call(
        functools.partial(token_kernel, slots, sources),
        out_shape=(piece,) * sources + (jax.ShapeDtypeStruct((2, count), jnp.int32),),
        in_specs=[hbm] * 2,
        out_specs=(vmem,) * (sources + 1),
        scratch_shapes=[pltpu.VMEM((2, count), jnp.int32), pltpu.VMEM((count, width), BF16), sems((2,))],
        compiler_params=params(),
        name="dispatch_tokens",
    )(ids_rows, tokens)
    win = weight_in.reshape(held, FF, width)
    wout = weight_out.reshape(held, FF, width)

    def exchange(stack):
        cut = stack.reshape(sources, 2 * slots, half)
        return lax.all_to_all(cut, "seq", split_axis=0, concat_axis=0, tiled=True).reshape(stacked, half)

    def regroup(*stacks):
        return vmem_call(
            functools.partial(regroup_kernel, slots, held, sources),
            rows_shape,
            stacks,
            "regroup",
            cost(product, 4 * stacked * half),
        )

    def across(rows, axis, bit):
        return lax.ppermute(rows, axis, [(i, i ^ bit) for i in range(lax.axis_size(axis))])

    def from_peers(rows, first):
        got, bit = [rows, first], far // 2
        while bit:
            got = got + [across(one, "dp", bit) for one in got]
            bit = bit // 2
        return got

    far = groups // 2
    arrived = [pieces[0]] + [across(pieces[j], "seq", j) for j in range(1, sources)]
    send_d = pl.pallas_call(
        functools.partial(cotangent_kernel, slots),
        out_shape=slab,
        in_specs=[vmem, vmem, hbm],
        out_specs=vmem,
        scratch_shapes=[pltpu.VMEM((count, width), BF16), sems],
        compiler_params=params(),
        name="dispatch_cotangents",
    )(target, gate_rows, cotangent)
    order = (7,6,5,4,3,2,1)
    send_d, *moved = lax.optimization_barrier((send_d, *[arrived[j] for j in order]))
    for j, one in zip(order, moved):
        arrived[j] = one
    got_d = exchange(send_d)
    rows_x = regroup(*arrived)
    first_x = across(rows_x, "dp", far)

    units = pltpu.VMEM((held, per_expert, FF), BF16)
    experts = pltpu.VMEM((held, FF, width), BF16)
    send_out, act, slope = pl.pallas_call(
        functools.partial(forward_kernel, slots, held, sources),
        out_shape=(slab, units_shape, units_shape),
        in_specs=[vmem, hbm, hbm],
        out_specs=(vmem, hbm, hbm),
        scratch_shapes=[experts, experts, units, units, sems((4, held))],
        compiler_params=params(),
        cost_estimate=cost(4 * product, 4 * weight_in.size),
        name="expert_forward",
    )(rows_x, win, wout)
    got_out = exchange(send_out)
    first_x, rows_x, act = lax.optimization_barrier((first_x, rows_x, act))
    rows_d = regroup(got_d)
    first_d = across(rows_d, "dp", far)
    all_x = from_peers(rows_x, first_x)
    send_in, dhid = pl.pallas_call(
        functools.partial(backward_kernel, slots, held, sources),
        out_shape=(slab, units_shape),
        in_specs=[vmem, hbm, hbm, hbm],
        out_specs=(vmem, hbm),
        scratch_shapes=[experts, experts, units, units, sems((4, held))],
        compiler_params=params(),
        cost_estimate=cost(4 * product, 4 * weight_in.size),
        name="expert_backward",
    )(rows_d, slope, wout, win)
    send_in, *all_x = lax.optimization_barrier((send_in, *all_x))
    first_d, rows_d, dhid = lax.optimization_barrier((first_d, rows_d, dhid))
    got_in = exchange(send_in)
    all_d = from_peers(rows_d, first_d)

    share = width // groups
    index = lax.axis_index("dp").astype(jnp.int32).reshape(1)
    gradient = jax.ShapeDtypeStruct((share, held * FF), F32)
    parts = 1
    some = FF // parts
    gradient_spec = pl.BlockSpec((share, some), lambda k, f, index: (0, k * parts + f))
    cut = pl.BlockSpec((1, per_expert, share), lambda k, f, index: (k, 0, index[0]))
    full = pl.BlockSpec((1, per_expert, width), lambda k, f, index: (k, 0, 0))
    own = pl.BlockSpec((1, per_expert, some), lambda k, f, index: (k, 0, f))
    weights = pl.BlockSpec((1, some, width), lambda k, f, index: (k, f, 0))
    weight_in_grad, weight_out_grad = pl.pallas_call(
        functools.partial(gradient_kernel, peers, factor),
        out_shape=(gradient, gradient),
        grid_spec=pltpu.PrefetchScalarGridSpec(
            num_scalar_prefetch=1,
            grid=(held, parts),
            in_specs=[cut, cut, own, own, weights, weights] + [full] * (2 * peers),
            out_specs=(gradient_spec, gradient_spec),
        ),
        compiler_params=params(),
        cost_estimate=cost(12 * product, 8 * weight_in.size),
        name="gradients",
    )(index, rows_x, rows_d, act, dhid, win, wout, *all_x[1:], *all_d[1:])

    layer_out, gate_grad = vmem_call(
        functools.partial(output_kernel, slots),
        (jax.ShapeDtypeStruct((count, width), BF16), jax.ShapeDtypeStruct((2, count), F32)),
        [target, gate_rows, cotangent, got_out],
        "combine_output",
    )
    got_in, weight_in_grad = lax.optimization_barrier((got_in, weight_in_grad))
    input_grad = vmem_call(
        functools.partial(input_kernel, slots),
        jax.ShapeDtypeStruct((count, width), BF16),
        [target, got_in],
        "combine_input",
    )
    return layer_out, gate_grad.T, input_grad, weight_in_grad, weight_out_grad


def slot_numbers(ids_block):
    flat_ids = ids_block.reshape(-1)
    onehot = (flat_ids[:, None] == jnp.arange(E, dtype=jnp.int32)[None, :]).astype(jnp.int32)
    before = jnp.cumsum(onehot, axis=0) - onehot
    return jnp.sum(before * onehot, axis=1).reshape(ids_block.shape)


def local_sums(tokens, gate_values, expert_ids, cotangent, weight_in, weight_out):
    seq_count = lax.axis_size("seq")
    group_count = lax.axis_size("dp")
    own_units = weight_in.shape[0]
    block_units = min(FF, own_units)
    held_experts = own_units // block_units
    block_count = FF // block_units
    tok_count = tokens.shape[0]
    model_width = tokens.shape[1]
    factor = (E / (2.0 * tok_count * seq_count * group_count)) ** 0.5
    row_total = seq_count * CAP
    slot_of = slot_numbers(expert_ids)
    flat_target = (expert_ids * CAP + slot_of).reshape(-1)
    token_of = jnp.repeat(jnp.arange(tok_count, dtype=jnp.int32), 2)
    slot_token = jnp.zeros((E * CAP,), jnp.int32).at[flat_target].set(token_of)
    slot_used = jnp.zeros((E * CAP,), jnp.float32).at[flat_target].set(1.0)
    slot_gate = jnp.zeros((E * CAP,), jnp.float32).at[flat_target].set(gate_values.reshape(-1))
    column = np.arange(seq_count * held_experts * CAP)
    owner_of = column // (held_experts * CAP)
    local_of = column // CAP % held_experts
    expert_of = (owner_of * own_units + local_of * block_units) // FF
    code_table = jnp.asarray(expert_of * CAP + column % CAP, dtype=jnp.int32)
    col_token = slot_token[code_table]
    col_used = slot_used[code_table]
    col_gate = slot_gate[code_table]
    send_shape = (seq_count, held_experts * CAP, model_width)
    send_x = (
        (tokens[col_token].astype(jnp.float32) * col_used[:, None])
        .astype(jnp.bfloat16)
        .reshape(send_shape)
    )
    send_d = (
        (cotangent[col_token].astype(jnp.float32) * col_gate[:, None])
        .astype(jnp.bfloat16)
        .reshape(send_shape)
    )
    win_local = weight_in.reshape(held_experts, block_units, model_width)
    wout_local = weight_out.reshape(held_experts, block_units, model_width)

    def to_rows(arrived):
        grouped = arrived.reshape(seq_count, held_experts, CAP, model_width)
        return jnp.transpose(grouped, (1, 0, 2, 3)).reshape(held_experts, row_total, model_width)

    def from_rows(results):
        grouped = results.reshape(held_experts, seq_count, CAP, model_width)
        return jnp.transpose(grouped, (1, 0, 2, 3)).reshape(send_shape)

    rows_x = to_rows(lax.all_to_all(send_x, "seq", split_axis=0, concat_axis=0, tiled=True))
    hidden = jnp.einsum("krd,kfd->krf", rows_x, win_local, preferred_element_type=jnp.float32)
    act = gelu_value(hidden).astype(jnp.bfloat16)
    part_out = jnp.einsum(
        "krf,kfd->krd", act, wout_local, preferred_element_type=jnp.float32
    ).astype(jnp.bfloat16)
    back_out = lax.all_to_all(from_rows(part_out), "seq", split_axis=0, concat_axis=0, tiled=True)
    rows_d = to_rows(lax.all_to_all(send_d, "seq", split_axis=0, concat_axis=0, tiled=True))
    back_hidden = jnp.einsum("krd,kfd->krf", rows_d, wout_local, preferred_element_type=jnp.float32)
    dhid = (back_hidden * gelu_slope(hidden)).astype(jnp.bfloat16)
    part_in = jnp.einsum(
        "krf,kfd->krd", dhid, win_local, preferred_element_type=jnp.float32
    ).astype(jnp.bfloat16)
    back_in = lax.all_to_all(from_rows(part_in), "seq", split_axis=0, concat_axis=0, tiled=True)

    def collect(returned):
        flat_rows = returned.reshape(-1, model_width)
        summed = jnp.zeros((tok_count, 2, model_width), jnp.float32)
        for block_index in range(block_count):
            unit_start = expert_ids * FF + block_index * block_units
            row_at = (
                unit_start // own_units * (held_experts * CAP)
                + unit_start % own_units // block_units * CAP
                + slot_of
            )
            summed = summed + flat_rows[row_at].astype(jnp.float32)
        return summed

    expert_out = collect(back_out)
    layer_out = jnp.sum(gate_values[:, :, None] * expert_out, axis=1).astype(jnp.bfloat16)
    gate_grad = jnp.sum(cotangent.astype(jnp.float32)[:, None, :] * expert_out, axis=2)
    input_grad = jnp.sum(collect(back_in), axis=1).astype(jnp.bfloat16)
    x_columns = jnp.transpose(rows_x, (2, 0, 1))
    d_columns = jnp.transpose(rows_d, (2, 0, 1))
    grad_in_part = (
        jnp.einsum("dkr,krf->dkf", x_columns, dhid, preferred_element_type=jnp.float32).reshape(
            model_width, own_units
        )
        * factor
    )
    grad_out_part = (
        jnp.einsum("dkr,krf->dkf", d_columns, act, preferred_element_type=jnp.float32).reshape(
            model_width, own_units
        )
        * factor
    )
    summed_grads = lax.psum_scatter(
        jnp.concatenate([grad_in_part, grad_out_part], axis=1).astype(jnp.bfloat16),
        "dp",
        scatter_dimension=0,
        tiled=True,
    ).astype(jnp.float32)
    weight_in_grad = summed_grads[:, :own_units]
    weight_out_grad = summed_grads[:, own_units:]
    return (layer_out, gate_grad, input_grad, weight_in_grad, weight_out_grad)


def local(tokens, gate_values, expert_ids, cotangent, weight_in, weight_out):
    units = weight_in.shape[0]
    sources, groups = lax.axis_size("seq"), lax.axis_size("dp")
    row_values = sources * max(units // FF, 1) * CAP * groups
    paired = sources & (sources - 1) == 0 and groups & (groups - 1) == 0 and groups > 1
    plan = local_rows if units % FF == 0 and row_values < units and paired else local_sums
    return plan(tokens, gate_values, expert_ids, cotangent, weight_in, weight_out)


def solution(mesh):
    in_specs = (
        P(("dp", "seq"), None),
        P(("dp", "seq"), None),
        P(("dp", "seq"), None),
        P(("dp", "seq"), None),
        P("seq", None),
        P("seq", None),
    )
    out_specs = (
        P(("dp", "seq"), None),
        P(("dp", "seq"), None),
        P(("dp", "seq"), None),
        P("dp", "seq"),
        P("dp", "seq"),
    )
    return jax.shard_map(local, mesh=mesh, in_specs=in_specs, out_specs=out_specs, check_vma=False)
```

```python
import functools

import jax
import jax.numpy as jnp
import numpy as np
from jax import lax
from jax.experimental import pallas as pl
from jax.experimental.pallas import tpu as pltpu
from jax.sharding import PartitionSpec as P

E = 32
FF = 1024
CAP = 9

BF16 = jnp.bfloat16
F32 = jnp.float32

gelu_scale = 0.7978845608028654
gelu_cubic = 0.044715


def gelu_value(values):
    inner_arg = gelu_scale * (values + gelu_cubic * values * values * values)
    return 0.5 * values * (1.0 + jnp.tanh(inner_arg))


def gelu_slope(values):
    inner_arg = gelu_scale * (values + gelu_cubic * values * values * values)
    tanh_val = jnp.tanh(inner_arg)
    return 0.5 * (1.0 + tanh_val) + 0.5 * values * (1.0 - tanh_val * tanh_val) * gelu_scale * (
        1.0 + 3.0 * gelu_cubic * values * values
    )


def gelu_both(values):
    square = values * values
    tanh_val = jnp.tanh(gelu_scale * (values + gelu_cubic * square * values))
    half_up = 0.5 * (1.0 + tanh_val)
    slope = half_up + 0.5 * values * (1.0 - tanh_val * tanh_val) * gelu_scale * (
        1.0 + 3.0 * gelu_cubic * square
    )
    return values * half_up, slope


def iota(shape, dim):
    return lax.broadcasted_iota(jnp.int32, shape, dim)


def quotient(numbers, divisor):
    return jnp.floor((numbers.astype(F32) + 0.5) * (1.0 / divisor)).astype(jnp.int32)


def dot(a, b, dims):
    return lax.dot_general(a, b, ((dims[0], dims[1]), ((), ())), preferred_element_type=F32)


def ones_where(mask):
    return jnp.where(mask, 1.0, 0.0).astype(BF16)


def slab_slot(numbers, slots):
    slab = quotient(numbers, 2 * slots)
    rest = numbers - slab * (2 * slots)
    right = rest >= slots
    return slab, jnp.where(right, rest - slots, rest), right


def here(axis):
    return lax.axis_index(axis).astype(jnp.int32)


def token_kernel(slots, sources, ids_hbm, tok_hbm, *refs):
    slab_refs, (target_ref, ids_ref, tok_ref, sems) = refs[:sources], refs[sources:]
    ids_copy = pltpu.make_async_copy(ids_hbm, ids_ref, sems.at[0])
    tok_copy = pltpu.make_async_copy(tok_hbm, tok_ref, sems.at[1])
    ids_copy.start()
    tok_copy.start()
    count = tok_ref.shape[0]
    half = tok_ref.shape[1] // 2
    expert = iota((E, count), 0)
    earlier = ones_where(iota((count, count), 0) < iota((count, count), 1))
    slab, slot, right = slab_slot(iota((sources * 2 * slots, 1), 0), slots)
    slot = (slab ^ here("seq")) * slots + slot
    ids_copy.wait()
    ids = ids_ref[...]
    first, second = ids[0:1, :], ids[1:2, :]
    hot_first, hot_second = expert == first, expert == second
    before = dot(ones_where(hot_first | hot_second), earlier, ((1,), (0,)))
    slot_first = jnp.sum(jnp.where(hot_first, before, 0.0), axis=0, keepdims=True)
    slot_second = jnp.sum(jnp.where(hot_second, before, 0.0), axis=0, keepdims=True)
    target_first = first * CAP + slot_first.astype(jnp.int32)
    target_second = second * CAP + slot_second.astype(jnp.int32)
    target_ref[0:1, :] = target_first
    target_ref[1:2, :] = target_second
    pick = ones_where((slot == target_first) | (slot == target_second))
    tok_copy.wait()
    rows = dot(pick, tok_ref[...], ((1,), (0,)))
    rows = jnp.where(right, rows[:, half:], rows[:, :half]).astype(BF16)
    for j, slab_ref in enumerate(slab_refs):
        slab_ref[...] = rows[j * 2 * slots : (j + 1) * 2 * slots]


def cotangent_kernel(slots, mask, target_ref, gate_ref, cot_hbm, slab_ref, cot_ref, sem):
    copy = pltpu.make_async_copy(cot_hbm, cot_ref, sem)
    copy.start()
    half = cot_ref.shape[1] // 2
    slab, slot, right = slab_slot(iota((slab_ref.shape[0], 1), 0), slots)
    slot = (slab ^ mask) * slots + slot
    is_first, is_second = slot == target_ref[0:1, :], slot == target_ref[1:2, :]
    gate = jnp.sum(
        jnp.where(is_first, gate_ref[0:1, :], 0.0) + jnp.where(is_second, gate_ref[1:2, :], 0.0),
        axis=1,
        keepdims=True,
    )
    copy.wait()
    rows = dot(ones_where(is_first | is_second), cot_ref[...], ((1,), (0,)))
    slab_ref[...] = (jnp.where(right, rows[:, half:], rows[:, :half]) * gate).astype(BF16)


def regroup_kernel(slots, held, sources, mask, *refs):
    slab_refs, (rows_ref, own_ref, sem) = list(refs[:-3]), refs[-3:]
    own = pltpu.make_async_copy(slab_refs[0], own_ref, sem)
    own.start()
    slab_refs[0] = own_ref
    per_expert = sources * CAP
    half = own_ref.shape[1]
    number = iota((held * per_expert, 1), 0)
    expert = quotient(number, per_expert)
    rest = number - expert * per_expert
    source = quotient(rest, CAP)
    slab = source ^ (here("seq") if len(slab_refs) > 1 else mask)
    row = slab * (2 * slots) + expert * CAP + rest - source * CAP
    at = iota((held * per_expert, 2 * slots * sources), 1)
    own.wait()
    slabs = jnp.concatenate([ref[...] for ref in slab_refs], axis=0)
    for side in (0, 1):
        rows = dot(ones_where(at == row + side * slots), slabs, ((1,), (0,)))
        for k in range(held):
            span = slice(k * per_expert, (k + 1) * per_expert)
            rows_ref[k, :, side * half : (side + 1) * half] = rows[span].astype(BF16)


def send_slabs(parts, slots, held, sources, mask, out_hbm, out_ref, sems):
    per_expert = sources * CAP
    rows = jnp.concatenate(parts, axis=0).astype(BF16)
    half = rows.shape[1] // 2
    size = slots * sources
    copies = []
    for piece in (0, 1):
        span = pl.ds(piece * size, size)
        source, slot, right = slab_slot(iota((size, 1), 0) + piece * size, slots)
        expert = quotient(slot, CAP)
        row = expert * per_expert + (source ^ mask) * CAP + slot - expert * CAP
        out = dot(ones_where(iota((size, held * per_expert), 1) == row), rows, ((1,), (0,)))
        out_ref[span] = jnp.where(right, out[:, half:], out[:, :half]).astype(BF16)
        copies.append(pltpu.make_async_copy(out_ref.at[span], out_hbm.at[span], sems.at[piece]))
        copies[piece].start()
    return copies


def loads_of(sources_and_targets, sems):
    copies = []
    for i, (there, near) in enumerate(sources_and_targets):
        copies.append([pltpu.make_async_copy(there.at[k], near.at[k], sems.at[i, k]) for k in range(near.shape[0])])
        for copy in copies[i]:
            copy.start()
    return copies


def forward_kernel(slots, held, sources, mask, rows_hbm, up_hbm, down_hbm, out_hbm, act_hbm, slope_hbm, *scratch):
    rows_ref, up_ref, down_ref, act_ref, slope_ref, out_ref, sems = scratch
    own, ups, downs = loads_of([(rows_hbm, rows_ref), (up_hbm, up_ref), (down_hbm, down_ref)], sems)
    stores = []

    def product(k):
        own[k].wait()
        ups[k].wait()
        return dot(rows_ref[k], up_ref[k], ((1,), (1,)))

    hidden = product(0)
    for k in range(held):
        now = hidden
        if k + 1 < held:
            hidden = product(k + 1)
        value, slope = gelu_both(now)
        act_ref[k] = value.astype(BF16)
        slope_ref[k] = slope.astype(BF16)
        for i, (near, there) in enumerate([(act_ref, act_hbm), (slope_ref, slope_hbm)]):
            stores.append(pltpu.make_async_copy(near.at[k], there.at[k], sems.at[3 + i, k]))
            stores[-1].start()
    parts = []
    for k in range(held):
        downs[k].wait()
        parts.append(dot(act_ref[k], down_ref[k], ((1,), (0,))))
    stores = stores + send_slabs(parts, slots, held, sources, mask, out_hbm, out_ref, sems.at[5])
    for store in stores:
        store.wait()


def backward_kernel(slots, held, sources, mask, rows_hbm, slope_hbm, up_hbm, down_hbm, out_hbm, dhid_hbm, *scratch):
    rows_ref, up_ref, down_ref, dhid_ref, slope_ref, out_ref, sems = scratch
    own, slopes, ups, downs = loads_of(
        [(rows_hbm, rows_ref), (slope_hbm, slope_ref), (up_hbm, up_ref), (down_hbm, down_ref)], sems
    )
    stores = []
    for k in range(held):
        own[k].wait()
        slopes[k].wait()
        ups[k].wait()
        back = dot(rows_ref[k], up_ref[k], ((1,), (1,)))
        dhid_ref[k] = (back * slope_ref[k].astype(F32)).astype(BF16)
        stores.append(pltpu.make_async_copy(dhid_ref.at[k], dhid_hbm.at[k], sems.at[4, k]))
        stores[-1].start()
    parts = []
    for k in range(held):
        downs[k].wait()
        parts.append(dot(dhid_ref[k], down_ref[k], ((1,), (0,))))
    stores = stores + send_slabs(parts, slots, held, sources, mask, out_hbm, out_ref, sems.at[5])
    for store in stores:
        store.wait()


def gradient_kernel(peers, factor, share_ref, *refs):
    own_x_ref, own_d_ref, act_ref, dhid_ref, up_ref, down_ref = refs[:6]
    x_refs, d_refs = refs[6 : 6 + peers], refs[6 + peers : 6 + 2 * peers]
    grad_in_ref, grad_out_ref = refs[6 + 2 * peers :]
    wide = grad_in_ref.shape[0]
    share = pl.ds(pl.multiple_of(share_ref[0] * wide, 128), wide)
    rows_x = jnp.concatenate([ref[0] for ref in x_refs], axis=0)
    rows_d = jnp.concatenate([ref[0] for ref in d_refs], axis=0)
    hidden = dot(rows_x, up_ref[0], ((1,), (1,)))
    back = dot(rows_d, down_ref[0], ((1,), (1,)))
    value, slope = gelu_both(hidden)
    acts = jnp.concatenate([act_ref[0], value.astype(BF16)], axis=0)
    cut_d = jnp.concatenate([own_d_ref[0]] + [ref[0, :, share] for ref in d_refs], axis=0)
    grad_out_ref[...] = dot(cut_d, acts, ((0,), (0,))) * factor
    dhids = jnp.concatenate([dhid_ref[0], (back * slope).astype(BF16)], axis=0)
    cut_x = jnp.concatenate([own_x_ref[0]] + [ref[0, :, share] for ref in x_refs], axis=0)
    grad_in_ref[...] = dot(cut_x, dhids, ((0,), (0,))) * factor


def as_column(row):
    count = row.shape[1]
    same = iota((count, count), 0) == iota((count, count), 1)
    return jnp.sum(jnp.where(same, row, 0.0), axis=1, keepdims=True)


def as_row(column):
    count = column.shape[0]
    same = iota((count, count), 0) == iota((count, count), 1)
    return jnp.sum(jnp.where(same, column, 0.0), axis=0, keepdims=True)


def picked(target_ref, slots, rows, mask):
    slab, slot, right = slab_slot(iota((1, rows), 1), slots)
    slot = (slab ^ mask) * slots + slot
    columns = [as_column(target_ref[k : k + 1, :].astype(F32)).astype(jnp.int32) for k in (0, 1)]
    return [[(slot == column) & ~right, (slot == column) & right] for column in columns]


def combine_kernel(slots, mask, target_ref, gate_ref, cot_ref, out_ref, in_ref, layer_ref, gate_grad_ref, input_ref):
    half = out_ref.shape[1]
    picks = picked(target_ref, slots, out_ref.shape[0], mask)
    outs, ins = out_ref[...], in_ref[...]
    gates = gate_ref[...]
    cot = cot_ref[...].astype(F32)
    layer, dots = [0.0, 0.0], []
    for k in (0, 1):
        gate = as_column(gates[k : k + 1, :])
        grad = 0.0
        for side in (0, 1):
            rows = dot(ones_where(picks[k][side]), outs, ((1,), (0,)))
            layer[side] = layer[side] + gate * rows
            part = cot[:, side * half : (side + 1) * half] * rows
            grad = grad + jnp.sum(part, axis=1, keepdims=True)
        dots.append(as_row(grad))
    gate_grad_ref[...] = jnp.concatenate(dots, axis=0)
    for side in (0, 1):
        span = slice(side * half, (side + 1) * half)
        layer_ref[:, span] = layer[side].astype(BF16)
        pick = ones_where(picks[0][side] | picks[1][side])
        input_ref[:, span] = dot(pick, ins, ((1,), (0,))).astype(BF16)


def params(mib=58):
    return pltpu.CompilerParams(vmem_limit_bytes=mib * 1024 * 1024)


def cost(flops, bytes_accessed):
    return pl.CostEstimate(flops=int(flops), bytes_accessed=int(bytes_accessed), transcendentals=0)


def local_rows(tokens, gate_values, expert_ids, cotangent, weight_in, weight_out):
    sources = lax.axis_size("seq")
    groups = lax.axis_size("dp")
    peers = groups - 1
    count, width = tokens.shape
    half = width // 2
    held = weight_in.shape[0] // FF
    slots = held * CAP
    per_expert = sources * CAP
    stacked = sources * 2 * slots
    factor = (E / (2.0 * count * sources * groups)) ** 0.5
    slab = jax.ShapeDtypeStruct((stacked, half), BF16)
    mask = sources // 4
    rows_shape = jax.ShapeDtypeStruct((held, per_expert, width), BF16)
    units_shape = jax.ShapeDtypeStruct((held, per_expert, FF), BF16)
    peers_shape = jax.ShapeDtypeStruct((held, peers * per_expert, FF), BF16)
    product = 2 * held * per_expert * FF * width
    vmem = pl.BlockSpec(memory_space=pltpu.VMEM)

    hbm = pl.BlockSpec(memory_space=pltpu.HBM)
    sems = pltpu.SemaphoreType.DMA

    def by_expert(shape):
        return pl.BlockSpec((1, *shape), lambda k, *_: (k, 0, 0))

    ids_rows, gate_rows = expert_ids.T, gate_values.T
    piece = jax.ShapeDtypeStruct((2 * slots, half), BF16)
    *pieces, target = pl.pallas_call(
        functools.partial(token_kernel, slots, sources),
        out_shape=(piece,) * sources + (jax.ShapeDtypeStruct((2, count), jnp.int32),),
        in_specs=[hbm] * 2,
        out_specs=(vmem,) * (sources + 1),
        scratch_shapes=[pltpu.VMEM((2, count), jnp.int32), pltpu.VMEM((count, width), BF16), sems((2,))],
        compiler_params=params(),
        name="dispatch_tokens",
    )(ids_rows, tokens)
    win = weight_in.reshape(held, FF, width)
    wout = weight_out.reshape(held, FF, width)

    def exchange(stack):
        cut = stack.reshape(sources, 2 * slots, half)
        order = [[j ^ mask for j in range(sources)]]
        got = lax.all_to_all(cut, "seq", split_axis=0, concat_axis=0, tiled=True, axis_index_groups=order)
        return got.reshape(stacked, half)

    def regroup(*stacks):
        return pl.pallas_call(
            functools.partial(regroup_kernel, slots, held, sources, mask),
            out_shape=rows_shape,
            in_specs=[pl.BlockSpec(memory_space=pl.ANY)] + [vmem] * (len(stacks) - 1),
            out_specs=vmem,
            scratch_shapes=[pltpu.VMEM(stacks[0].shape, BF16), sems],
            compiler_params=params(6),
            cost_estimate=cost(product, 4 * stacked * half),
            name="regroup",
        )(*stacks)

    def across(rows, axis, bit):
        return lax.ppermute(rows, axis, [(i, i ^ bit) for i in range(lax.axis_size(axis))])

    def from_peers(rows, first):
        got, bit = [rows, first], far // 2
        while bit:
            got = got + [across(one, "dp", bit) for one in got]
            bit = bit // 2
        return got

    far = groups // 2
    arrived = [pieces[0]] + [across(pieces[j], "seq", j) for j in range(1, sources)]
    send_d = pl.pallas_call(
        functools.partial(cotangent_kernel, slots, mask),
        out_shape=slab,
        in_specs=[vmem, vmem, hbm],
        out_specs=vmem,
        scratch_shapes=[pltpu.VMEM((count, width), BF16), sems],
        compiler_params=params(),
        name="dispatch_cotangents",
    )(target, gate_rows, cotangent)
    order = range(sources - 1, 0, -1)
    send_d, *moved = lax.optimization_barrier((send_d, *[arrived[j] for j in order]))
    for j, one in zip(order, moved):
        arrived[j] = one
    got_d = exchange(send_d)
    rows_x = regroup(*arrived)
    first_x = across(rows_x, "dp", far)

    units = pltpu.VMEM((held, per_expert, FF), BF16)
    experts = pltpu.VMEM((held, FF, width), BF16)
    near_rows = pltpu.VMEM((held, per_expert, width), BF16)
    near_slab = pltpu.VMEM((stacked, half), BF16)
    send_out, act, slope = pl.pallas_call(
        functools.partial(forward_kernel, slots, held, sources, mask),
        out_shape=(slab, units_shape, units_shape),
        in_specs=[hbm] * 3,
        out_specs=(hbm,) * 3,
        scratch_shapes=[near_rows, experts, experts, units, units, near_slab, sems((6, max(held, 2)))],
        compiler_params=params(),
        cost_estimate=cost(4 * product, 4 * weight_in.size),
        name="expert_forward",
    )(rows_x, win, wout)
    got_out = exchange(send_out)
    first_x, rows_x, act = lax.optimization_barrier((first_x, rows_x, act))
    rows_d = regroup(got_d)
    first_d = across(rows_d, "dp", far)
    all_x = from_peers(rows_x, first_x)
    send_in, dhid = pl.pallas_call(
        functools.partial(backward_kernel, slots, held, sources, mask),
        out_shape=(slab, units_shape),
        in_specs=[hbm] * 4,
        out_specs=(hbm,) * 2,
        scratch_shapes=[near_rows, experts, experts, units, units, near_slab, sems((6, max(held, 2)))],
        compiler_params=params(),
        cost_estimate=cost(4 * product, 4 * weight_in.size),
        name="expert_backward",
    )(rows_d, slope, wout, win)
    first_d, rows_d, dhid = lax.optimization_barrier((first_d, rows_d, dhid))
    got_in = exchange(send_in)
    all_d = from_peers(rows_d, first_d)

    share = width // groups
    index = lax.axis_index("dp").astype(jnp.int32).reshape(1)
    gradient = jax.ShapeDtypeStruct((share, held * FF), F32)
    parts = 1
    some = FF // parts
    gradient_spec = pl.BlockSpec((share, some), lambda k, f, index: (0, k * parts + f))
    cut = pl.BlockSpec((1, per_expert, share), lambda k, f, index: (k, 0, index[0]))
    full = pl.BlockSpec((1, per_expert, width), lambda k, f, index: (k, 0, 0))
    own = pl.BlockSpec((1, per_expert, some), lambda k, f, index: (k, 0, f))
    weights = pl.BlockSpec((1, some, width), lambda k, f, index: (k, f, 0))
    weight_in_grad, weight_out_grad = pl.pallas_call(
        functools.partial(gradient_kernel, peers, factor),
        out_shape=(gradient, gradient),
        grid_spec=pltpu.PrefetchScalarGridSpec(
            num_scalar_prefetch=1,
            grid=(held, parts),
            in_specs=[cut, cut, own, own, weights, weights] + [full] * (2 * peers),
            out_specs=(gradient_spec, gradient_spec),
        ),
        compiler_params=params(),
        cost_estimate=cost(12 * product, 8 * weight_in.size),
        name="gradients",
    )(index, rows_x, rows_d, act, dhid, win, wout, *all_x[1:], *all_d[1:])

    got_in, got_out, weight_in_grad = lax.optimization_barrier((got_in, got_out, weight_in_grad))
    token_shape = jax.ShapeDtypeStruct((count, width), BF16)
    layer_out, gate_grad, input_grad = pl.pallas_call(
        functools.partial(combine_kernel, slots, mask),
        out_shape=(token_shape, jax.ShapeDtypeStruct((2, count), F32), token_shape),
        in_specs=[vmem] * 5,
        out_specs=(vmem,) * 3,
        compiler_params=params(6),
        name="combine",
    )(target, gate_rows, cotangent, got_out, got_in)
    return layer_out, gate_grad.T, input_grad, weight_in_grad, weight_out_grad


def slot_numbers(ids_block):
    flat_ids = ids_block.reshape(-1)
    onehot = (flat_ids[:, None] == jnp.arange(E, dtype=jnp.int32)[None, :]).astype(jnp.int32)
    before = jnp.cumsum(onehot, axis=0) - onehot
    return jnp.sum(before * onehot, axis=1).reshape(ids_block.shape)


def local_sums(tokens, gate_values, expert_ids, cotangent, weight_in, weight_out):
    seq_count = lax.axis_size("seq")
    group_count = lax.axis_size("dp")
    own_units = weight_in.shape[0]
    block_units = min(FF, own_units)
    held_experts = own_units // block_units
    block_count = FF // block_units
    tok_count = tokens.shape[0]
    model_width = tokens.shape[1]
    factor = (E / (2.0 * tok_count * seq_count * group_count)) ** 0.5
    row_total = seq_count * CAP
    slot_of = slot_numbers(expert_ids)
    flat_target = (expert_ids * CAP + slot_of).reshape(-1)
    token_of = jnp.repeat(jnp.arange(tok_count, dtype=jnp.int32), 2)
    slot_token = jnp.zeros((E * CAP,), jnp.int32).at[flat_target].set(token_of)
    slot_used = jnp.zeros((E * CAP,), jnp.float32).at[flat_target].set(1.0)
    slot_gate = jnp.zeros((E * CAP,), jnp.float32).at[flat_target].set(gate_values.reshape(-1))
    column = np.arange(seq_count * held_experts * CAP)
    owner_of = column // (held_experts * CAP)
    local_of = column // CAP % held_experts
    expert_of = (owner_of * own_units + local_of * block_units) // FF
    code_table = jnp.asarray(expert_of * CAP + column % CAP, dtype=jnp.int32)
    col_token = slot_token[code_table]
    col_used = slot_used[code_table]
    col_gate = slot_gate[code_table]
    send_shape = (seq_count, held_experts * CAP, model_width)
    send_x = (
        (tokens[col_token].astype(jnp.float32) * col_used[:, None])
        .astype(jnp.bfloat16)
        .reshape(send_shape)
    )
    send_d = (
        (cotangent[col_token].astype(jnp.float32) * col_gate[:, None])
        .astype(jnp.bfloat16)
        .reshape(send_shape)
    )
    win_local = weight_in.reshape(held_experts, block_units, model_width)
    wout_local = weight_out.reshape(held_experts, block_units, model_width)

    def to_rows(arrived):
        grouped = arrived.reshape(seq_count, held_experts, CAP, model_width)
        return jnp.transpose(grouped, (1, 0, 2, 3)).reshape(held_experts, row_total, model_width)

    def from_rows(results):
        grouped = results.reshape(held_experts, seq_count, CAP, model_width)
        return jnp.transpose(grouped, (1, 0, 2, 3)).reshape(send_shape)

    rows_x = to_rows(lax.all_to_all(send_x, "seq", split_axis=0, concat_axis=0, tiled=True))
    hidden = jnp.einsum("krd,kfd->krf", rows_x, win_local, preferred_element_type=jnp.float32)
    act = gelu_value(hidden).astype(jnp.bfloat16)
    part_out = jnp.einsum(
        "krf,kfd->krd", act, wout_local, preferred_element_type=jnp.float32
    ).astype(jnp.bfloat16)
    back_out = lax.all_to_all(from_rows(part_out), "seq", split_axis=0, concat_axis=0, tiled=True)
    rows_d = to_rows(lax.all_to_all(send_d, "seq", split_axis=0, concat_axis=0, tiled=True))
    back_hidden = jnp.einsum("krd,kfd->krf", rows_d, wout_local, preferred_element_type=jnp.float32)
    dhid = (back_hidden * gelu_slope(hidden)).astype(jnp.bfloat16)
    part_in = jnp.einsum(
        "krf,kfd->krd", dhid, win_local, preferred_element_type=jnp.float32
    ).astype(jnp.bfloat16)
    back_in = lax.all_to_all(from_rows(part_in), "seq", split_axis=0, concat_axis=0, tiled=True)

    def collect(returned):
        flat_rows = returned.reshape(-1, model_width)
        summed = jnp.zeros((tok_count, 2, model_width), jnp.float32)
        for block_index in range(block_count):
            unit_start = expert_ids * FF + block_index * block_units
            row_at = (
                unit_start // own_units * (held_experts * CAP)
                + unit_start % own_units // block_units * CAP
                + slot_of
            )
            summed = summed + flat_rows[row_at].astype(jnp.float32)
        return summed

    expert_out = collect(back_out)
    layer_out = jnp.sum(gate_values[:, :, None] * expert_out, axis=1).astype(jnp.bfloat16)
    gate_grad = jnp.sum(cotangent.astype(jnp.float32)[:, None, :] * expert_out, axis=2)
    input_grad = jnp.sum(collect(back_in), axis=1).astype(jnp.bfloat16)
    x_columns = jnp.transpose(rows_x, (2, 0, 1))
    d_columns = jnp.transpose(rows_d, (2, 0, 1))
    grad_in_part = (
        jnp.einsum("dkr,krf->dkf", x_columns, dhid, preferred_element_type=jnp.float32).reshape(
            model_width, own_units
        )
        * factor
    )
    grad_out_part = (
        jnp.einsum("dkr,krf->dkf", d_columns, act, preferred_element_type=jnp.float32).reshape(
            model_width, own_units
        )
        * factor
    )
    summed_grads = lax.psum_scatter(
        jnp.concatenate([grad_in_part, grad_out_part], axis=1).astype(jnp.bfloat16),
        "dp",
        scatter_dimension=0,
        tiled=True,
    ).astype(jnp.float32)
    weight_in_grad = summed_grads[:, :own_units]
    weight_out_grad = summed_grads[:, own_units:]
    return (layer_out, gate_grad, input_grad, weight_in_grad, weight_out_grad)


def local(tokens, gate_values, expert_ids, cotangent, weight_in, weight_out):
    units = weight_in.shape[0]
    sources, groups = lax.axis_size("seq"), lax.axis_size("dp")
    row_values = sources * max(units // FF, 1) * CAP * groups
    paired = sources & (sources - 1) == 0 and groups & (groups - 1) == 0 and groups > 1
    plan = local_rows if units % FF == 0 and row_values < units and paired else local_sums
    return plan(tokens, gate_values, expert_ids, cotangent, weight_in, weight_out)


def solution(mesh):
    in_specs = (
        P(("dp", "seq"), None),
        P(("dp", "seq"), None),
        P(("dp", "seq"), None),
        P(("dp", "seq"), None),
        P("seq", None),
        P("seq", None),
    )
    out_specs = (
        P(("dp", "seq"), None),
        P(("dp", "seq"), None),
        P(("dp", "seq"), None),
        P("dp", "seq"),
        P("dp", "seq"),
    )
    return jax.shard_map(local, mesh=mesh, in_specs=in_specs, out_specs=out_specs, check_vma=False)
```

```python
import functools

import jax
import jax.numpy as jnp
import numpy as np
from jax import lax
from jax.experimental import pallas as pl
from jax.experimental.pallas import tpu as pltpu
from jax.sharding import PartitionSpec as P

E = 32
FF = 1024
CAP = 9

BF16 = jnp.bfloat16
F32 = jnp.float32

gelu_scale = 0.7978845608028654
gelu_cubic = 0.044715


def gelu_value(values):
    inner_arg = gelu_scale * (values + gelu_cubic * values * values * values)
    return 0.5 * values * (1.0 + jnp.tanh(inner_arg))


def gelu_slope(values):
    inner_arg = gelu_scale * (values + gelu_cubic * values * values * values)
    tanh_val = jnp.tanh(inner_arg)
    return 0.5 * (1.0 + tanh_val) + 0.5 * values * (1.0 - tanh_val * tanh_val) * gelu_scale * (
        1.0 + 3.0 * gelu_cubic * values * values
    )


def gelu_both(values):
    square = values * values
    tanh_val = jnp.tanh(gelu_scale * (values + gelu_cubic * square * values))
    half_up = 0.5 * (1.0 + tanh_val)
    slope = half_up + 0.5 * values * (1.0 - tanh_val * tanh_val) * gelu_scale * (
        1.0 + 3.0 * gelu_cubic * square
    )
    return values * half_up, slope


def iota(shape, dim):
    return lax.broadcasted_iota(jnp.int32, shape, dim)


def quotient(numbers, divisor):
    return jnp.floor((numbers.astype(F32) + 0.5) * (1.0 / divisor)).astype(jnp.int32)


def dot(a, b, dims):
    return lax.dot_general(a, b, ((dims[0], dims[1]), ((), ())), preferred_element_type=F32)


def ones_where(mask):
    return jnp.where(mask, 1.0, 0.0).astype(BF16)


def slab_slot(numbers, slots):
    slab = quotient(numbers, 2 * slots)
    rest = numbers - slab * (2 * slots)
    right = rest >= slots
    return slab, jnp.where(right, rest - slots, rest), right


def here(axis):
    return lax.axis_index(axis).astype(jnp.int32)


def token_kernel(slots, sources, ids_hbm, gate_hbm, tok_hbm, *refs):
    slab_refs, (target_ref, ids_ref, gate_ref, tok_ref, sems) = refs[: sources - 1], refs[sources - 1 :]
    gate_copy = pltpu.make_async_copy(gate_hbm, gate_ref, sems.at[2])
    ids_copy = pltpu.make_async_copy(ids_hbm, ids_ref, sems.at[0])
    tok_copy = pltpu.make_async_copy(tok_hbm, tok_ref, sems.at[1])
    ids_copy.start()
    tok_copy.start()
    gate_copy.start()
    count = tok_ref.shape[0]
    half = tok_ref.shape[1] // 2
    expert = iota((E, count), 0)
    earlier = ones_where(iota((count, count), 0) < iota((count, count), 1))
    slab, slot, right = slab_slot(iota((sources * 2 * slots, 1), 0), slots)
    slot = (slab ^ here("seq")) * slots + slot
    ids_copy.wait()
    ids = ids_ref[...]
    first, second = ids[0:1, :], ids[1:2, :]
    hot_first, hot_second = expert == first, expert == second
    before = dot(ones_where(hot_first | hot_second), earlier, ((1,), (0,)))
    slot_first = jnp.sum(jnp.where(hot_first, before, 0.0), axis=0, keepdims=True)
    slot_second = jnp.sum(jnp.where(hot_second, before, 0.0), axis=0, keepdims=True)
    target_first = first * CAP + slot_first.astype(jnp.int32)
    target_second = second * CAP + slot_second.astype(jnp.int32)
    gate_copy.wait()
    target_ref[0:1, :] = target_first.astype(F32)
    target_ref[1:2, :] = target_second.astype(F32)
    target_ref[2:4, :] = gate_ref[...]
    pick = ones_where((slot == target_first) | (slot == target_second))
    tok_copy.wait()
    rows = dot(pick, tok_ref[...], ((1,), (0,)))
    rows = jnp.where(right, rows[:, half:], rows[:, :half]).astype(BF16)
    for j, slab_ref in enumerate(slab_refs):
        slab_ref[...] = rows[(j + 1) * 2 * slots : (j + 2) * 2 * slots]


def cotangent_kernel(slots, mask, target_ref, cot_ref, tok_ref, slab_ref, own_ref):
    half = cot_ref.shape[1] // 2
    targets = target_ref[0:2, :].astype(jnp.int32)
    slab, slot, right = slab_slot(iota((slab_ref.shape[0], 1), 0), slots)
    slot = (slab ^ mask) * slots + slot
    is_first, is_second = slot == targets[0:1, :], slot == targets[1:2, :]
    gate = jnp.sum(
        jnp.where(is_first, target_ref[2:3, :], 0.0) + jnp.where(is_second, target_ref[3:4, :], 0.0),
        axis=1,
        keepdims=True,
    )
    rows = dot(ones_where(is_first | is_second), cot_ref[...], ((1,), (0,)))
    slab_ref[...] = (jnp.where(right, rows[:, half:], rows[:, :half]) * gate).astype(BF16)
    slab, slot, right = slab_slot(iota((own_ref.shape[0], 1), 0), slots)
    slot = here("seq") * slots + slot
    pick = ones_where((slot == targets[0:1, :]) | (slot == targets[1:2, :]))
    rows = dot(pick, tok_ref[...], ((1,), (0,)))
    own_ref[...] = jnp.where(right, rows[:, half:], rows[:, :half]).astype(BF16)


def regroup_kernel(slots, held, sources, mask, *refs):
    slab_refs, rows_ref = refs[:-1], refs[-1]
    per_expert = sources * CAP
    half = slab_refs[0].shape[1]
    number = iota((held * per_expert, 1), 0)
    expert = quotient(number, per_expert)
    rest = number - expert * per_expert
    source = quotient(rest, CAP)
    slab = source ^ (here("seq") if len(slab_refs) > 1 else mask)
    row = slab * (2 * slots) + expert * CAP + rest - source * CAP
    at = iota((held * per_expert, 2 * slots * sources), 1)
    slabs = jnp.concatenate([ref[...] for ref in slab_refs], axis=0)
    for side in (0, 1):
        rows = dot(ones_where(at == row + side * slots), slabs, ((1,), (0,)))
        for k in range(held):
            span = slice(k * per_expert, (k + 1) * per_expert)
            rows_ref[k, :, side * half : (side + 1) * half] = rows[span].astype(BF16)


def send_slabs(parts, slots, held, sources, mask, out_hbm, out_ref, sems):
    per_expert = sources * CAP
    rows = jnp.concatenate(parts, axis=0).astype(BF16)
    half = rows.shape[1] // 2
    size = slots * sources
    copies = []
    for piece in (0, 1):
        span = pl.ds(piece * size, size)
        source, slot, right = slab_slot(iota((size, 1), 0) + piece * size, slots)
        expert = quotient(slot, CAP)
        row = expert * per_expert + (source ^ mask) * CAP + slot - expert * CAP
        out = dot(ones_where(iota((size, held * per_expert), 1) == row), rows, ((1,), (0,)))
        out_ref[span] = jnp.where(right, out[:, half:], out[:, :half]).astype(BF16)
        copies.append(pltpu.make_async_copy(out_ref.at[span], out_hbm.at[span], sems.at[piece]))
        copies[piece].start()
    return copies


def loads_of(sources_and_targets, sems):
    copies = []
    for i, (there, near) in enumerate(sources_and_targets):
        copies.append([pltpu.make_async_copy(there.at[k], near.at[k], sems.at[i, k]) for k in range(near.shape[0])])
        for copy in copies[i]:
            copy.start()
    return copies


def forward_kernel(slots, held, sources, mask, rows_hbm, up_hbm, down_hbm, out_hbm, act_hbm, slope_hbm, *scratch):
    rows_ref, up_ref, down_ref, act_ref, slope_ref, out_ref, sems = scratch
    own, ups, downs = loads_of([(rows_hbm, rows_ref), (up_hbm, up_ref), (down_hbm, down_ref)], sems)
    stores = []

    def product(k):
        own[k].wait()
        ups[k].wait()
        return dot(rows_ref[k], up_ref[k], ((1,), (1,)))

    hidden = product(0)
    for k in range(held):
        now = hidden
        if k + 1 < held:
            hidden = product(k + 1)
        value, slope = gelu_both(now)
        act_ref[k] = value.astype(BF16)
        slope_ref[k] = slope.astype(BF16)
        for i, (near, there) in enumerate([(act_ref, act_hbm), (slope_ref, slope_hbm)]):
            stores.append(pltpu.make_async_copy(near.at[k], there.at[k], sems.at[3 + i, k]))
            stores[-1].start()
    parts = []
    for k in range(held):
        downs[k].wait()
        parts.append(dot(act_ref[k], down_ref[k], ((1,), (0,))))
    stores = stores + send_slabs(parts, slots, held, sources, mask, out_hbm, out_ref, sems.at[5])
    for store in stores:
        store.wait()


def backward_kernel(slots, held, sources, mask, rows_hbm, slope_hbm, up_hbm, down_hbm, out_hbm, dhid_hbm, *scratch):
    rows_ref, up_ref, down_ref, dhid_ref, slope_ref, out_ref, sems = scratch
    own, slopes, ups, downs = loads_of(
        [(rows_hbm, rows_ref), (slope_hbm, slope_ref), (up_hbm, up_ref), (down_hbm, down_ref)], sems
    )
    stores = []
    for k in range(held):
        own[k].wait()
        slopes[k].wait()
        ups[k].wait()
        back = dot(rows_ref[k], up_ref[k], ((1,), (1,)))
        dhid_ref[k] = (back * slope_ref[k].astype(F32)).astype(BF16)
        stores.append(pltpu.make_async_copy(dhid_ref.at[k], dhid_hbm.at[k], sems.at[4, k]))
        stores[-1].start()
    parts = []
    for k in range(held):
        downs[k].wait()
        parts.append(dot(dhid_ref[k], down_ref[k], ((1,), (0,))))
    stores = stores + send_slabs(parts, slots, held, sources, mask, out_hbm, out_ref, sems.at[5])
    for store in stores:
        store.wait()


def gradient_kernel(peers, factor, share_ref, *refs):
    own_x_ref, own_d_ref, act_ref, dhid_ref, up_ref, down_ref = refs[:6]
    x_refs, d_refs = refs[6 : 6 + peers], refs[6 + peers : 6 + 2 * peers]
    grad_in_ref, grad_out_ref = refs[6 + 2 * peers :]
    wide = grad_in_ref.shape[0]
    share = pl.ds(pl.multiple_of(share_ref[0] * wide, 128), wide)
    rows_x = jnp.concatenate([ref[0] for ref in x_refs], axis=0)
    rows_d = jnp.concatenate([ref[0] for ref in d_refs], axis=0)
    hidden = dot(rows_x, up_ref[0], ((1,), (1,)))
    back = dot(rows_d, down_ref[0], ((1,), (1,)))
    value, slope = gelu_both(hidden)
    acts = jnp.concatenate([act_ref[0], value.astype(BF16)], axis=0)
    cut_d = jnp.concatenate([own_d_ref[0]] + [ref[0, :, share] for ref in d_refs], axis=0)
    grad_out_ref[...] = dot(cut_d, acts, ((0,), (0,))) * factor
    dhids = jnp.concatenate([dhid_ref[0], (back * slope).astype(BF16)], axis=0)
    cut_x = jnp.concatenate([own_x_ref[0]] + [ref[0, :, share] for ref in x_refs], axis=0)
    grad_in_ref[...] = dot(cut_x, dhids, ((0,), (0,))) * factor


def as_column(row):
    count = row.shape[1]
    same = iota((count, count), 0) == iota((count, count), 1)
    return jnp.sum(jnp.where(same, row, 0.0), axis=1, keepdims=True)


def as_row(column):
    count = column.shape[0]
    same = iota((count, count), 0) == iota((count, count), 1)
    return jnp.sum(jnp.where(same, column, 0.0), axis=0, keepdims=True)


def picked(target_ref, slots, rows, mask):
    slab, slot, right = slab_slot(iota((1, rows), 1), slots)
    slot = (slab ^ mask) * slots + slot
    columns = [as_column(target_ref[k : k + 1, :]).astype(jnp.int32) for k in (0, 1)]
    return [[(slot == column) & ~right, (slot == column) & right] for column in columns]


def combine_kernel(slots, mask, target_ref, cot_ref, out_ref, in_ref, layer_ref, gate_grad_ref, input_ref):
    half = out_ref.shape[1]
    picks = picked(target_ref, slots, out_ref.shape[0], mask)
    outs, ins = out_ref[...], in_ref[...]
    gates = target_ref[2:4, :]
    cot = cot_ref[...].astype(F32)
    layer, dots = [0.0, 0.0], []
    for k in (0, 1):
        gate = as_column(gates[k : k + 1, :])
        grad = 0.0
        for side in (0, 1):
            rows = dot(ones_where(picks[k][side]), outs, ((1,), (0,)))
            layer[side] = layer[side] + gate * rows
            part = cot[:, side * half : (side + 1) * half] * rows
            grad = grad + jnp.sum(part, axis=1, keepdims=True)
        dots.append(as_row(grad))
    gate_grad_ref[...] = jnp.concatenate(dots, axis=0)
    for side in (0, 1):
        span = slice(side * half, (side + 1) * half)
        layer_ref[:, span] = layer[side].astype(BF16)
        pick = ones_where(picks[0][side] | picks[1][side])
        input_ref[:, span] = dot(pick, ins, ((1,), (0,))).astype(BF16)


def params(mib=58):
    return pltpu.CompilerParams(vmem_limit_bytes=mib * 1024 * 1024)


def cost(flops, bytes_accessed):
    return pl.CostEstimate(flops=int(flops), bytes_accessed=int(bytes_accessed), transcendentals=0)


def local_rows(tokens, gate_values, expert_ids, cotangent, weight_in, weight_out):
    sources = lax.axis_size("seq")
    groups = lax.axis_size("dp")
    peers = groups - 1
    count, width = tokens.shape
    half = width // 2
    held = weight_in.shape[0] // FF
    slots = held * CAP
    per_expert = sources * CAP
    stacked = sources * 2 * slots
    factor = (E / (2.0 * count * sources * groups)) ** 0.5
    slab = jax.ShapeDtypeStruct((stacked, half), BF16)
    mask = sources // 4
    rows_shape = jax.ShapeDtypeStruct((held, per_expert, width), BF16)
    units_shape = jax.ShapeDtypeStruct((held, per_expert, FF), BF16)
    peers_shape = jax.ShapeDtypeStruct((held, peers * per_expert, FF), BF16)
    product = 2 * held * per_expert * FF * width
    vmem = pl.BlockSpec(memory_space=pltpu.VMEM)

    hbm = pl.BlockSpec(memory_space=pltpu.HBM)
    sems = pltpu.SemaphoreType.DMA

    def by_expert(shape):
        return pl.BlockSpec((1, *shape), lambda k, *_: (k, 0, 0))

    ids_rows, gate_rows = expert_ids.T, gate_values.T
    piece = jax.ShapeDtypeStruct((2 * slots, half), BF16)
    *pieces, target = pl.pallas_call(
        functools.partial(token_kernel, slots, sources),
        out_shape=(piece,) * (sources - 1) + (jax.ShapeDtypeStruct((4, count), F32),),
        in_specs=[hbm] * 3,
        out_specs=(vmem,) * sources,
        scratch_shapes=[
            pltpu.VMEM((2, count), jnp.int32),
            pltpu.VMEM((2, count), F32),
            pltpu.VMEM((count, width), BF16),
            sems((3,)),
        ],
        compiler_params=params(),
        name="dispatch_tokens",
    )(ids_rows, gate_rows, tokens)
    win = weight_in.reshape(held, FF, width)
    wout = weight_out.reshape(held, FF, width)

    def exchange(stack):
        cut = stack.reshape(sources, 2 * slots, half)
        order = [[j ^ mask for j in range(sources)]]
        got = lax.all_to_all(cut, "seq", split_axis=0, concat_axis=0, tiled=True, axis_index_groups=order)
        return got.reshape(stacked, half)

    def regroup(*stacks):
        return pl.pallas_call(
            functools.partial(regroup_kernel, slots, held, sources, mask),
            out_shape=rows_shape,
            in_specs=[vmem] * len(stacks),
            out_specs=vmem,
            compiler_params=params(6),
            cost_estimate=cost(product, 4 * stacked * half),
            name="regroup",
        )(*stacks)

    def across(rows, axis, bit):
        return lax.ppermute(rows, axis, [(i, i ^ bit) for i in range(lax.axis_size(axis))])

    def from_peers(rows, first):
        got, bit = [rows, first], far // 2
        while bit:
            got = got + [across(one, "dp", bit) for one in got]
            bit = bit // 2
        return got

    far = groups // 2
    send_d, own_piece = pl.pallas_call(
        functools.partial(cotangent_kernel, slots, mask),
        out_shape=(slab, piece),
        in_specs=[vmem] * 3,
        out_specs=(vmem, vmem),
        compiler_params=params(6),
        name="dispatch_cotangents",
    )(target, cotangent, tokens)
    arrived = [own_piece] + [across(pieces[j - 1], "seq", j) for j in range(1, sources)]
    order = range(sources - 1, 0, -1)
    send_d, *moved = lax.optimization_barrier((send_d, *[arrived[j] for j in order]))
    for j, one in zip(order, moved):
        arrived[j] = one
    got_d = exchange(send_d)
    rows_x = regroup(*arrived)
    first_x = across(rows_x, "dp", far)

    units = pltpu.VMEM((held, per_expert, FF), BF16)
    experts = pltpu.VMEM((held, FF, width), BF16)
    near_rows = pltpu.VMEM((held, per_expert, width), BF16)
    near_slab = pltpu.VMEM((stacked, half), BF16)
    send_out, act, slope = pl.pallas_call(
        functools.partial(forward_kernel, slots, held, sources, mask),
        out_shape=(slab, units_shape, units_shape),
        in_specs=[hbm] * 3,
        out_specs=(hbm,) * 3,
        scratch_shapes=[near_rows, experts, experts, units, units, near_slab, sems((6, max(held, 2)))],
        compiler_params=params(),
        cost_estimate=cost(4 * product, 4 * weight_in.size),
        name="expert_forward",
    )(rows_x, win, wout)
    got_out = exchange(send_out)
    first_x, rows_x, act = lax.optimization_barrier((first_x, rows_x, act))
    rows_d = regroup(got_d)
    first_d = across(rows_d, "dp", far)
    all_x = from_peers(rows_x, first_x)
    send_in, dhid = pl.pallas_call(
        functools.partial(backward_kernel, slots, held, sources, mask),
        out_shape=(slab, units_shape),
        in_specs=[hbm] * 4,
        out_specs=(hbm,) * 2,
        scratch_shapes=[near_rows, experts, experts, units, units, near_slab, sems((6, max(held, 2)))],
        compiler_params=params(),
        cost_estimate=cost(4 * product, 4 * weight_in.size),
        name="expert_backward",
    )(rows_d, slope, wout, win)
    first_d, rows_d, dhid = lax.optimization_barrier((first_d, rows_d, dhid))
    got_in = exchange(send_in)
    all_d = from_peers(rows_d, first_d)

    share = width // groups
    index = lax.axis_index("dp").astype(jnp.int32).reshape(1)
    gradient = jax.ShapeDtypeStruct((share, held * FF), F32)
    parts = 1
    some = FF // parts
    gradient_spec = pl.BlockSpec((share, some), lambda k, f, index: (0, k * parts + f))
    cut = pl.BlockSpec((1, per_expert, share), lambda k, f, index: (k, 0, index[0]))
    full = pl.BlockSpec((1, per_expert, width), lambda k, f, index: (k, 0, 0))
    own = pl.BlockSpec((1, per_expert, some), lambda k, f, index: (k, 0, f))
    weights = pl.BlockSpec((1, some, width), lambda k, f, index: (k, f, 0))
    weight_in_grad, weight_out_grad = pl.pallas_call(
        functools.partial(gradient_kernel, peers, factor),
        out_shape=(gradient, gradient),
        grid_spec=pltpu.PrefetchScalarGridSpec(
            num_scalar_prefetch=1,
            grid=(held, parts),
            in_specs=[cut, cut, own, own, weights, weights] + [full] * (2 * peers),
            out_specs=(gradient_spec, gradient_spec),
        ),
        compiler_params=params(),
        cost_estimate=cost(12 * product, 8 * weight_in.size),
        name="gradients",
    )(index, rows_x, rows_d, act, dhid, win, wout, *all_x[1:], *all_d[1:])

    got_in, got_out, weight_in_grad = lax.optimization_barrier((got_in, got_out, weight_in_grad))
    token_shape = jax.ShapeDtypeStruct((count, width), BF16)
    layer_out, gate_grad, input_grad = pl.pallas_call(
        functools.partial(combine_kernel, slots, mask),
        out_shape=(token_shape, jax.ShapeDtypeStruct((2, count), F32), token_shape),
        in_specs=[vmem] * 4,
        out_specs=(vmem,) * 3,
        compiler_params=params(6),
        name="combine",
    )(target, cotangent, got_out, got_in)
    return layer_out, gate_grad.T, input_grad, weight_in_grad, weight_out_grad


def slot_numbers(ids_block):
    flat_ids = ids_block.reshape(-1)
    onehot = (flat_ids[:, None] == jnp.arange(E, dtype=jnp.int32)[None, :]).astype(jnp.int32)
    before = jnp.cumsum(onehot, axis=0) - onehot
    return jnp.sum(before * onehot, axis=1).reshape(ids_block.shape)


def local_sums(tokens, gate_values, expert_ids, cotangent, weight_in, weight_out):
    seq_count = lax.axis_size("seq")
    group_count = lax.axis_size("dp")
    own_units = weight_in.shape[0]
    block_units = min(FF, own_units)
    held_experts = own_units // block_units
    block_count = FF // block_units
    tok_count = tokens.shape[0]
    model_width = tokens.shape[1]
    factor = (E / (2.0 * tok_count * seq_count * group_count)) ** 0.5
    row_total = seq_count * CAP
    slot_of = slot_numbers(expert_ids)
    flat_target = (expert_ids * CAP + slot_of).reshape(-1)
    token_of = jnp.repeat(jnp.arange(tok_count, dtype=jnp.int32), 2)
    slot_token = jnp.zeros((E * CAP,), jnp.int32).at[flat_target].set(token_of)
    slot_used = jnp.zeros((E * CAP,), jnp.float32).at[flat_target].set(1.0)
    slot_gate = jnp.zeros((E * CAP,), jnp.float32).at[flat_target].set(gate_values.reshape(-1))
    column = np.arange(seq_count * held_experts * CAP)
    owner_of = column // (held_experts * CAP)
    local_of = column // CAP % held_experts
    expert_of = (owner_of * own_units + local_of * block_units) // FF
    code_table = jnp.asarray(expert_of * CAP + column % CAP, dtype=jnp.int32)
    col_token = slot_token[code_table]
    col_used = slot_used[code_table]
    col_gate = slot_gate[code_table]
    send_shape = (seq_count, held_experts * CAP, model_width)
    send_x = (
        (tokens[col_token].astype(jnp.float32) * col_used[:, None])
        .astype(jnp.bfloat16)
        .reshape(send_shape)
    )
    send_d = (
        (cotangent[col_token].astype(jnp.float32) * col_gate[:, None])
        .astype(jnp.bfloat16)
        .reshape(send_shape)
    )
    win_local = weight_in.reshape(held_experts, block_units, model_width)
    wout_local = weight_out.reshape(held_experts, block_units, model_width)

    def to_rows(arrived):
        grouped = arrived.reshape(seq_count, held_experts, CAP, model_width)
        return jnp.transpose(grouped, (1, 0, 2, 3)).reshape(held_experts, row_total, model_width)

    def from_rows(results):
        grouped = results.reshape(held_experts, seq_count, CAP, model_width)
        return jnp.transpose(grouped, (1, 0, 2, 3)).reshape(send_shape)

    rows_x = to_rows(lax.all_to_all(send_x, "seq", split_axis=0, concat_axis=0, tiled=True))
    hidden = jnp.einsum("krd,kfd->krf", rows_x, win_local, preferred_element_type=jnp.float32)
    act = gelu_value(hidden).astype(jnp.bfloat16)
    part_out = jnp.einsum(
        "krf,kfd->krd", act, wout_local, preferred_element_type=jnp.float32
    ).astype(jnp.bfloat16)
    back_out = lax.all_to_all(from_rows(part_out), "seq", split_axis=0, concat_axis=0, tiled=True)
    rows_d = to_rows(lax.all_to_all(send_d, "seq", split_axis=0, concat_axis=0, tiled=True))
    back_hidden = jnp.einsum("krd,kfd->krf", rows_d, wout_local, preferred_element_type=jnp.float32)
    dhid = (back_hidden * gelu_slope(hidden)).astype(jnp.bfloat16)
    part_in = jnp.einsum(
        "krf,kfd->krd", dhid, win_local, preferred_element_type=jnp.float32
    ).astype(jnp.bfloat16)
    back_in = lax.all_to_all(from_rows(part_in), "seq", split_axis=0, concat_axis=0, tiled=True)

    def collect(returned):
        flat_rows = returned.reshape(-1, model_width)
        summed = jnp.zeros((tok_count, 2, model_width), jnp.float32)
        for block_index in range(block_count):
            unit_start = expert_ids * FF + block_index * block_units
            row_at = (
                unit_start // own_units * (held_experts * CAP)
                + unit_start % own_units // block_units * CAP
                + slot_of
            )
            summed = summed + flat_rows[row_at].astype(jnp.float32)
        return summed

    expert_out = collect(back_out)
    layer_out = jnp.sum(gate_values[:, :, None] * expert_out, axis=1).astype(jnp.bfloat16)
    gate_grad = jnp.sum(cotangent.astype(jnp.float32)[:, None, :] * expert_out, axis=2)
    input_grad = jnp.sum(collect(back_in), axis=1).astype(jnp.bfloat16)
    x_columns = jnp.transpose(rows_x, (2, 0, 1))
    d_columns = jnp.transpose(rows_d, (2, 0, 1))
    grad_in_part = (
        jnp.einsum("dkr,krf->dkf", x_columns, dhid, preferred_element_type=jnp.float32).reshape(
            model_width, own_units
        )
        * factor
    )
    grad_out_part = (
        jnp.einsum("dkr,krf->dkf", d_columns, act, preferred_element_type=jnp.float32).reshape(
            model_width, own_units
        )
        * factor
    )
    summed_grads = lax.psum_scatter(
        jnp.concatenate([grad_in_part, grad_out_part], axis=1).astype(jnp.bfloat16),
        "dp",
        scatter_dimension=0,
        tiled=True,
    ).astype(jnp.float32)
    weight_in_grad = summed_grads[:, :own_units]
    weight_out_grad = summed_grads[:, own_units:]
    return (layer_out, gate_grad, input_grad, weight_in_grad, weight_out_grad)


def local(tokens, gate_values, expert_ids, cotangent, weight_in, weight_out):
    units = weight_in.shape[0]
    sources, groups = lax.axis_size("seq"), lax.axis_size("dp")
    row_values = sources * max(units // FF, 1) * CAP * groups
    paired = sources & (sources - 1) == 0 and groups & (groups - 1) == 0 and groups > 1
    plan = local_rows if units % FF == 0 and row_values < units and paired else local_sums
    return plan(tokens, gate_values, expert_ids, cotangent, weight_in, weight_out)


def solution(mesh):
    in_specs = (
        P(("dp", "seq"), None),
        P(("dp", "seq"), None),
        P(("dp", "seq"), None),
        P(("dp", "seq"), None),
        P("seq", None),
        P("seq", None),
    )
    out_specs = (
        P(("dp", "seq"), None),
        P(("dp", "seq"), None),
        P(("dp", "seq"), None),
        P("dp", "seq"),
        P("dp", "seq"),
    )
    return jax.shard_map(local, mesh=mesh, in_specs=in_specs, out_specs=out_specs, check_vma=False)
```

```python
import functools

import jax
import jax.numpy as jnp
import numpy as np
from jax import lax
from jax.experimental import pallas as pl
from jax.experimental.pallas import tpu as pltpu
from jax.sharding import PartitionSpec as P

E = 32
FF = 1024
CAP = 9

BF16 = jnp.bfloat16
F32 = jnp.float32

gelu_scale = 0.7978845608028654
gelu_cubic = 0.044715


def gelu_value(values):
    inner_arg = gelu_scale * (values + gelu_cubic * values * values * values)
    return 0.5 * values * (1.0 + jnp.tanh(inner_arg))


def gelu_slope(values):
    inner_arg = gelu_scale * (values + gelu_cubic * values * values * values)
    tanh_val = jnp.tanh(inner_arg)
    return 0.5 * (1.0 + tanh_val) + 0.5 * values * (1.0 - tanh_val * tanh_val) * gelu_scale * (
        1.0 + 3.0 * gelu_cubic * values * values
    )


def gelu_both(values):
    square = values * values
    tanh_val = jnp.tanh(gelu_scale * (values + gelu_cubic * square * values))
    half_up = 0.5 * (1.0 + tanh_val)
    slope = half_up + 0.5 * values * (1.0 - tanh_val * tanh_val) * gelu_scale * (
        1.0 + 3.0 * gelu_cubic * square
    )
    return values * half_up, slope


def iota(shape, dim):
    return lax.broadcasted_iota(jnp.int32, shape, dim)


def quotient(numbers, divisor):
    return jnp.floor((numbers.astype(F32) + 0.5) * (1.0 / divisor)).astype(jnp.int32)


def dot(a, b, dims):
    return lax.dot_general(a, b, ((dims[0], dims[1]), ((), ())), preferred_element_type=F32)


def ones_where(mask):
    return jnp.where(mask, 1.0, 0.0).astype(BF16)


def slab_slot(numbers, slots):
    slab = quotient(numbers, 2 * slots)
    rest = numbers - slab * (2 * slots)
    right = rest >= slots
    return slab, jnp.where(right, rest - slots, rest), right


def here(axis):
    return lax.axis_index(axis).astype(jnp.int32)


def token_kernel(slots, sources, ids_hbm, gate_hbm, tok_hbm, *refs):
    slab_refs, (target_ref, ids_ref, gate_ref, tok_ref, sems) = refs[: sources - 1], refs[sources - 1 :]
    gate_copy = pltpu.make_async_copy(gate_hbm, gate_ref, sems.at[2])
    ids_copy = pltpu.make_async_copy(ids_hbm, ids_ref, sems.at[0])
    tok_copy = pltpu.make_async_copy(tok_hbm, tok_ref, sems.at[1])
    ids_copy.start()
    tok_copy.start()
    gate_copy.start()
    count = tok_ref.shape[0]
    half = tok_ref.shape[1] // 2
    expert = iota((E, count), 0)
    earlier = ones_where(iota((count, count), 0) < iota((count, count), 1))
    slab, slot, right = slab_slot(iota((sources * 2 * slots, 1), 0), slots)
    slot = (slab ^ here("seq")) * slots + slot
    ids_copy.wait()
    ids = ids_ref[...]
    first, second = ids[0:1, :], ids[1:2, :]
    hot_first, hot_second = expert == first, expert == second
    before = dot(ones_where(hot_first | hot_second), earlier, ((1,), (0,)))
    slot_first = jnp.sum(jnp.where(hot_first, before, 0.0), axis=0, keepdims=True)
    slot_second = jnp.sum(jnp.where(hot_second, before, 0.0), axis=0, keepdims=True)
    target_first = first * CAP + slot_first.astype(jnp.int32)
    target_second = second * CAP + slot_second.astype(jnp.int32)
    gate_copy.wait()
    target_ref[0:1, :] = target_first.astype(F32)
    target_ref[1:2, :] = target_second.astype(F32)
    target_ref[2:4, :] = gate_ref[...]
    pick = ones_where((slot == target_first) | (slot == target_second))
    tok_copy.wait()
    rows = dot(pick, tok_ref[...], ((1,), (0,)))
    rows = jnp.where(right, rows[:, half:], rows[:, :half]).astype(BF16)
    for j, slab_ref in enumerate(slab_refs):
        slab_ref[...] = rows[(j + 1) * 2 * slots : (j + 2) * 2 * slots]


def cotangent_kernel(slots, mask, target_ref, cot_ref, tok_ref, slab_ref, own_ref):
    half = cot_ref.shape[1] // 2
    targets = target_ref[0:2, :].astype(jnp.int32)
    slab, slot, right = slab_slot(iota((slab_ref.shape[0], 1), 0), slots)
    slot = (slab ^ mask) * slots + slot
    is_first, is_second = slot == targets[0:1, :], slot == targets[1:2, :]
    gate = jnp.sum(
        jnp.where(is_first, target_ref[2:3, :], 0.0) + jnp.where(is_second, target_ref[3:4, :], 0.0),
        axis=1,
        keepdims=True,
    )
    rows = dot(ones_where(is_first | is_second), cot_ref[...], ((1,), (0,)))
    slab_ref[...] = (jnp.where(right, rows[:, half:], rows[:, :half]) * gate).astype(BF16)
    slab, slot, right = slab_slot(iota((own_ref.shape[0], 1), 0), slots)
    slot = here("seq") * slots + slot
    pick = ones_where((slot == targets[0:1, :]) | (slot == targets[1:2, :]))
    rows = dot(pick, tok_ref[...], ((1,), (0,)))
    own_ref[...] = jnp.where(right, rows[:, half:], rows[:, :half]).astype(BF16)


def regroup_kernel(slots, held, sources, mask, *refs):
    slab_refs, rows_ref = refs[:-1], refs[-1]
    per_expert = sources * CAP
    half = slab_refs[0].shape[1]
    number = iota((held * per_expert, 1), 0)
    expert = quotient(number, per_expert)
    rest = number - expert * per_expert
    source = quotient(rest, CAP)
    slab = source ^ (here("seq") if len(slab_refs) > 1 else mask)
    row = slab * (2 * slots) + expert * CAP + rest - source * CAP
    at = iota((held * per_expert, 2 * slots * sources), 1)
    slabs = jnp.concatenate([ref[...] for ref in slab_refs], axis=0)
    for side in (0, 1):
        rows = dot(ones_where(at == row + side * slots), slabs, ((1,), (0,)))
        for k in range(held):
            span = slice(k * per_expert, (k + 1) * per_expert)
            rows_ref[k, :, side * half : (side + 1) * half] = rows[span].astype(BF16)


def send_slabs(parts, slots, held, sources, mask, out_hbm, out_ref, sems):
    per_expert = sources * CAP
    rows = jnp.concatenate(parts, axis=0).astype(BF16)
    half = rows.shape[1] // 2
    size = slots * sources
    copies = []
    for piece in (0, 1):
        span = pl.ds(piece * size, size)
        source, slot, right = slab_slot(iota((size, 1), 0) + piece * size, slots)
        expert = quotient(slot, CAP)
        row = expert * per_expert + (source ^ mask) * CAP + slot - expert * CAP
        out = dot(ones_where(iota((size, held * per_expert), 1) == row), rows, ((1,), (0,)))
        out_ref[span] = jnp.where(right, out[:, half:], out[:, :half]).astype(BF16)
        copies.append(pltpu.make_async_copy(out_ref.at[span], out_hbm.at[span], sems.at[piece]))
        copies[piece].start()
    return copies


def loads_of(sources_and_targets, sems):
    copies = []
    for i, (there, near) in enumerate(sources_and_targets):
        copies.append([pltpu.make_async_copy(there.at[k], near.at[k], sems.at[i, k]) for k in range(near.shape[0])])
        for copy in copies[i]:
            copy.start()
    return copies


def forward_kernel(slots, held, sources, mask, rows_hbm, up_hbm, down_hbm, out_hbm, act_hbm, slope_hbm, *scratch):
    rows_ref, up_ref, down_ref, act_ref, slope_ref, out_ref, sems = scratch
    own, ups, downs = loads_of([(rows_hbm, rows_ref), (up_hbm, up_ref), (down_hbm, down_ref)], sems)
    stores = []

    for k in range(held):
        own[k].wait()
        ups[k].wait()
        value, slope = gelu_both(dot(rows_ref[k], up_ref[k], ((1,), (1,))))
        act_ref[k] = value.astype(BF16)
        slope_ref[k] = slope.astype(BF16)
        for i, (near, there) in enumerate([(act_ref, act_hbm), (slope_ref, slope_hbm)]):
            stores.append(pltpu.make_async_copy(near.at[k], there.at[k], sems.at[3 + i, k]))
            stores[-1].start()
    parts = []
    for k in range(held):
        downs[k].wait()
        parts.append(dot(act_ref[k], down_ref[k], ((1,), (0,))))
    stores = stores + send_slabs(parts, slots, held, sources, mask, out_hbm, out_ref, sems.at[5])
    for store in stores:
        store.wait()


def backward_kernel(slots, held, sources, mask, rows_hbm, slope_hbm, up_hbm, down_hbm, out_hbm, dhid_hbm, *scratch):
    rows_ref, up_ref, down_ref, dhid_ref, slope_ref, out_ref, sems = scratch
    own, slopes, ups, downs = loads_of(
        [(rows_hbm, rows_ref), (slope_hbm, slope_ref), (up_hbm, up_ref), (down_hbm, down_ref)], sems
    )
    stores = []
    for k in range(held):
        own[k].wait()
        slopes[k].wait()
        ups[k].wait()
        back = dot(rows_ref[k], up_ref[k], ((1,), (1,)))
        dhid_ref[k] = (back * slope_ref[k].astype(F32)).astype(BF16)
        stores.append(pltpu.make_async_copy(dhid_ref.at[k], dhid_hbm.at[k], sems.at[4, k]))
        stores[-1].start()
    parts = []
    for k in range(held):
        downs[k].wait()
        parts.append(dot(dhid_ref[k], down_ref[k], ((1,), (0,))))
    stores = stores + send_slabs(parts, slots, held, sources, mask, out_hbm, out_ref, sems.at[5])
    for store in stores:
        store.wait()


def gradient_kernel(peers, factor, share_ref, *refs):
    own_x_ref, own_d_ref, act_ref, dhid_ref, up_ref, down_ref = refs[:6]
    x_refs, d_refs = refs[6 : 6 + peers], refs[6 + peers : 6 + 2 * peers]
    grad_in_ref, grad_out_ref = refs[6 + 2 * peers :]
    wide = grad_in_ref.shape[0]
    share = pl.ds(pl.multiple_of(share_ref[0] * wide, 128), wide)
    rows_x = jnp.concatenate([ref[0] for ref in x_refs], axis=0)
    rows_d = jnp.concatenate([ref[0] for ref in d_refs], axis=0)
    hidden = dot(rows_x, up_ref[0], ((1,), (1,)))
    back = dot(rows_d, down_ref[0], ((1,), (1,)))
    value, slope = gelu_both(hidden)
    acts = jnp.concatenate([act_ref[0], value.astype(BF16)], axis=0)
    cut_d = jnp.concatenate([own_d_ref[0]] + [ref[0, :, share] for ref in d_refs], axis=0)
    grad_out_ref[...] = dot(cut_d, acts, ((0,), (0,))) * factor
    dhids = jnp.concatenate([dhid_ref[0], (back * slope).astype(BF16)], axis=0)
    cut_x = jnp.concatenate([own_x_ref[0]] + [ref[0, :, share] for ref in x_refs], axis=0)
    grad_in_ref[...] = dot(cut_x, dhids, ((0,), (0,))) * factor


def as_column(row):
    count = row.shape[1]
    same = iota((count, count), 0) == iota((count, count), 1)
    return jnp.sum(jnp.where(same, row, 0.0), axis=1, keepdims=True)


def as_row(column):
    count = column.shape[0]
    same = iota((count, count), 0) == iota((count, count), 1)
    return jnp.sum(jnp.where(same, column, 0.0), axis=0, keepdims=True)


def picked(target_ref, slots, rows, mask):
    slab, slot, right = slab_slot(iota((1, rows), 1), slots)
    slot = (slab ^ mask) * slots + slot
    columns = [as_column(target_ref[k : k + 1, :]).astype(jnp.int32) for k in (0, 1)]
    return [[(slot == column) & ~right, (slot == column) & right] for column in columns]


def combine_kernel(slots, mask, target_ref, cot_ref, out_ref, in_ref, layer_ref, gate_grad_ref, input_ref):
    half = out_ref.shape[1]
    picks = picked(target_ref, slots, out_ref.shape[0], mask)
    outs, ins = out_ref[...], in_ref[...]
    gates = target_ref[2:4, :]
    cot = cot_ref[...].astype(F32)
    layer, dots = [0.0, 0.0], []
    for k in (0, 1):
        gate = as_column(gates[k : k + 1, :])
        grad = 0.0
        for side in (0, 1):
            rows = dot(ones_where(picks[k][side]), outs, ((1,), (0,)))
            layer[side] = layer[side] + gate * rows
            part = cot[:, side * half : (side + 1) * half] * rows
            grad = grad + jnp.sum(part, axis=1, keepdims=True)
        dots.append(as_row(grad))
    gate_grad_ref[...] = jnp.concatenate(dots, axis=0)
    for side in (0, 1):
        span = slice(side * half, (side + 1) * half)
        layer_ref[:, span] = layer[side].astype(BF16)
        pick = ones_where(picks[0][side] | picks[1][side])
        input_ref[:, span] = dot(pick, ins, ((1,), (0,))).astype(BF16)


def params(mib=58):
    return pltpu.CompilerParams(vmem_limit_bytes=mib * 1024 * 1024)


def cost(flops, bytes_accessed):
    return pl.CostEstimate(flops=int(flops), bytes_accessed=int(bytes_accessed), transcendentals=0)


def local_rows(tokens, gate_values, expert_ids, cotangent, weight_in, weight_out):
    sources = lax.axis_size("seq")
    groups = lax.axis_size("dp")
    peers = groups - 1
    count, width = tokens.shape
    half = width // 2
    held = weight_in.shape[0] // FF
    slots = held * CAP
    per_expert = sources * CAP
    stacked = sources * 2 * slots
    factor = (E / (2.0 * count * sources * groups)) ** 0.5
    slab = jax.ShapeDtypeStruct((stacked, half), BF16)
    mask = sources // 4
    rows_shape = jax.ShapeDtypeStruct((held, per_expert, width), BF16)
    units_shape = jax.ShapeDtypeStruct((held, per_expert, FF), BF16)
    peers_shape = jax.ShapeDtypeStruct((held, peers * per_expert, FF), BF16)
    product = 2 * held * per_expert * FF * width
    vmem = pl.BlockSpec(memory_space=pltpu.VMEM)

    hbm = pl.BlockSpec(memory_space=pltpu.HBM)
    sems = pltpu.SemaphoreType.DMA

    def by_expert(shape):
        return pl.BlockSpec((1, *shape), lambda k, *_: (k, 0, 0))

    ids_rows, gate_rows = expert_ids.T, gate_values.T
    piece = jax.ShapeDtypeStruct((2 * slots, half), BF16)
    *pieces, target = pl.pallas_call(
        functools.partial(token_kernel, slots, sources),
        out_shape=(piece,) * (sources - 1) + (jax.ShapeDtypeStruct((4, count), F32),),
        in_specs=[hbm] * 3,
        out_specs=(vmem,) * sources,
        scratch_shapes=[
            pltpu.VMEM((2, count), jnp.int32),
            pltpu.VMEM((2, count), F32),
            pltpu.VMEM((count, width), BF16),
            sems((3,)),
        ],
        compiler_params=params(),
        name="dispatch_tokens",
    )(ids_rows, gate_rows, tokens)
    win = weight_in.reshape(held, FF, width)
    wout = weight_out.reshape(held, FF, width)

    def exchange(stack):
        cut = stack.reshape(sources, 2 * slots, half)
        order = [[j ^ mask for j in range(sources)]]
        got = lax.all_to_all(cut, "seq", split_axis=0, concat_axis=0, tiled=True, axis_index_groups=order)
        return got.reshape(stacked, half)

    def regroup(*stacks):
        return pl.pallas_call(
            functools.partial(regroup_kernel, slots, held, sources, mask),
            out_shape=rows_shape,
            in_specs=[vmem] * len(stacks),
            out_specs=vmem,
            compiler_params=params(6),
            cost_estimate=cost(product, 4 * stacked * half),
            name="regroup",
        )(*stacks)

    def across(rows, axis, bit):
        return lax.ppermute(rows, axis, [(i, i ^ bit) for i in range(lax.axis_size(axis))])

    def from_peers(rows, first):
        got, bit = [rows, first], far // 2
        while bit:
            got = got + [across(one, "dp", bit) for one in got]
            bit = bit // 2
        return got

    far = groups // 2
    send_d, own_piece = pl.pallas_call(
        functools.partial(cotangent_kernel, slots, mask),
        out_shape=(slab, piece),
        in_specs=[vmem] * 3,
        out_specs=(vmem, vmem),
        compiler_params=params(6),
        name="dispatch_cotangents",
    )(target, cotangent, tokens)
    arrived = [own_piece] + [across(pieces[j - 1], "seq", j) for j in range(1, sources)]
    order = range(sources - 1, 0, -1)
    send_d, *moved = lax.optimization_barrier((send_d, *[arrived[j] for j in order]))
    for j, one in zip(order, moved):
        arrived[j] = one
    got_d = exchange(send_d)
    rows_x = regroup(*arrived)
    first_x = across(rows_x, "dp", far)

    units = pltpu.VMEM((held, per_expert, FF), BF16)
    experts = pltpu.VMEM((held, FF, width), BF16)
    near_rows = pltpu.VMEM((held, per_expert, width), BF16)
    near_slab = pltpu.VMEM((stacked, half), BF16)
    send_out, act, slope = pl.pallas_call(
        functools.partial(forward_kernel, slots, held, sources, mask),
        out_shape=(slab, units_shape, units_shape),
        in_specs=[hbm] * 3,
        out_specs=(hbm,) * 3,
        scratch_shapes=[near_rows, experts, experts, units, units, near_slab, sems((6, max(held, 2)))],
        compiler_params=params(),
        cost_estimate=cost(4 * product, 4 * weight_in.size),
        name="expert_forward",
    )(rows_x, win, wout)
    got_out = exchange(send_out)
    first_x, rows_x, act = lax.optimization_barrier((first_x, rows_x, act))
    rows_d = regroup(got_d)
    first_d = across(rows_d, "dp", far)
    all_x = from_peers(rows_x, first_x)
    send_in, dhid = pl.pallas_call(
        functools.partial(backward_kernel, slots, held, sources, mask),
        out_shape=(slab, units_shape),
        in_specs=[hbm] * 4,
        out_specs=(hbm,) * 2,
        scratch_shapes=[near_rows, experts, experts, units, units, near_slab, sems((6, max(held, 2)))],
        compiler_params=params(),
        cost_estimate=cost(4 * product, 4 * weight_in.size),
        name="expert_backward",
    )(rows_d, slope, wout, win)
    first_d, rows_d, dhid = lax.optimization_barrier((first_d, rows_d, dhid))
    got_in = exchange(send_in)
    all_d = from_peers(rows_d, first_d)

    share = width // groups
    index = lax.axis_index("dp").astype(jnp.int32).reshape(1)
    gradient = jax.ShapeDtypeStruct((share, held * FF), F32)
    parts = 1
    some = FF // parts
    gradient_spec = pl.BlockSpec((share, some), lambda k, f, index: (0, k * parts + f))
    cut = pl.BlockSpec((1, per_expert, share), lambda k, f, index: (k, 0, index[0]))
    full = pl.BlockSpec((1, per_expert, width), lambda k, f, index: (k, 0, 0))
    own = pl.BlockSpec((1, per_expert, some), lambda k, f, index: (k, 0, f))
    weights = pl.BlockSpec((1, some, width), lambda k, f, index: (k, f, 0))
    weight_in_grad, weight_out_grad = pl.pallas_call(
        functools.partial(gradient_kernel, peers, factor),
        out_shape=(gradient, gradient),
        grid_spec=pltpu.PrefetchScalarGridSpec(
            num_scalar_prefetch=1,
            grid=(held, parts),
            in_specs=[cut, cut, own, own, weights, weights] + [full] * (2 * peers),
            out_specs=(gradient_spec, gradient_spec),
        ),
        compiler_params=params(),
        cost_estimate=cost(12 * product, 8 * weight_in.size),
        name="gradients",
    )(index, rows_x, rows_d, act, dhid, win, wout, *all_x[1:], *all_d[1:])

    got_in, got_out, weight_in_grad = lax.optimization_barrier((got_in, got_out, weight_in_grad))
    token_shape = jax.ShapeDtypeStruct((count, width), BF16)
    layer_out, gate_grad, input_grad = pl.pallas_call(
        functools.partial(combine_kernel, slots, mask),
        out_shape=(token_shape, jax.ShapeDtypeStruct((2, count), F32), token_shape),
        in_specs=[vmem] * 4,
        out_specs=(vmem,) * 3,
        compiler_params=params(6),
        name="combine",
    )(target, cotangent, got_out, got_in)
    return layer_out, gate_grad.T, input_grad, weight_in_grad, weight_out_grad


def slot_numbers(ids_block):
    flat_ids = ids_block.reshape(-1)
    onehot = (flat_ids[:, None] == jnp.arange(E, dtype=jnp.int32)[None, :]).astype(jnp.int32)
    before = jnp.cumsum(onehot, axis=0) - onehot
    return jnp.sum(before * onehot, axis=1).reshape(ids_block.shape)


def local_sums(tokens, gate_values, expert_ids, cotangent, weight_in, weight_out):
    seq_count = lax.axis_size("seq")
    group_count = lax.axis_size("dp")
    own_units = weight_in.shape[0]
    block_units = min(FF, own_units)
    held_experts = own_units // block_units
    block_count = FF // block_units
    tok_count = tokens.shape[0]
    model_width = tokens.shape[1]
    factor = (E / (2.0 * tok_count * seq_count * group_count)) ** 0.5
    row_total = seq_count * CAP
    slot_of = slot_numbers(expert_ids)
    flat_target = (expert_ids * CAP + slot_of).reshape(-1)
    token_of = jnp.repeat(jnp.arange(tok_count, dtype=jnp.int32), 2)
    slot_token = jnp.zeros((E * CAP,), jnp.int32).at[flat_target].set(token_of)
    slot_used = jnp.zeros((E * CAP,), jnp.float32).at[flat_target].set(1.0)
    slot_gate = jnp.zeros((E * CAP,), jnp.float32).at[flat_target].set(gate_values.reshape(-1))
    column = np.arange(seq_count * held_experts * CAP)
    owner_of = column // (held_experts * CAP)
    local_of = column // CAP % held_experts
    expert_of = (owner_of * own_units + local_of * block_units) // FF
    code_table = jnp.asarray(expert_of * CAP + column % CAP, dtype=jnp.int32)
    col_token = slot_token[code_table]
    col_used = slot_used[code_table]
    col_gate = slot_gate[code_table]
    send_shape = (seq_count, held_experts * CAP, model_width)
    send_x = (
        (tokens[col_token].astype(jnp.float32) * col_used[:, None])
        .astype(jnp.bfloat16)
        .reshape(send_shape)
    )
    send_d = (
        (cotangent[col_token].astype(jnp.float32) * col_gate[:, None])
        .astype(jnp.bfloat16)
        .reshape(send_shape)
    )
    win_local = weight_in.reshape(held_experts, block_units, model_width)
    wout_local = weight_out.reshape(held_experts, block_units, model_width)

    def to_rows(arrived):
        grouped = arrived.reshape(seq_count, held_experts, CAP, model_width)
        return jnp.transpose(grouped, (1, 0, 2, 3)).reshape(held_experts, row_total, model_width)

    def from_rows(results):
        grouped = results.reshape(held_experts, seq_count, CAP, model_width)
        return jnp.transpose(grouped, (1, 0, 2, 3)).reshape(send_shape)

    rows_x = to_rows(lax.all_to_all(send_x, "seq", split_axis=0, concat_axis=0, tiled=True))
    hidden = jnp.einsum("krd,kfd->krf", rows_x, win_local, preferred_element_type=jnp.float32)
    act = gelu_value(hidden).astype(jnp.bfloat16)
    part_out = jnp.einsum(
        "krf,kfd->krd", act, wout_local, preferred_element_type=jnp.float32
    ).astype(jnp.bfloat16)
    back_out = lax.all_to_all(from_rows(part_out), "seq", split_axis=0, concat_axis=0, tiled=True)
    rows_d = to_rows(lax.all_to_all(send_d, "seq", split_axis=0, concat_axis=0, tiled=True))
    back_hidden = jnp.einsum("krd,kfd->krf", rows_d, wout_local, preferred_element_type=jnp.float32)
    dhid = (back_hidden * gelu_slope(hidden)).astype(jnp.bfloat16)
    part_in = jnp.einsum(
        "krf,kfd->krd", dhid, win_local, preferred_element_type=jnp.float32
    ).astype(jnp.bfloat16)
    back_in = lax.all_to_all(from_rows(part_in), "seq", split_axis=0, concat_axis=0, tiled=True)

    def collect(returned):
        flat_rows = returned.reshape(-1, model_width)
        summed = jnp.zeros((tok_count, 2, model_width), jnp.float32)
        for block_index in range(block_count):
            unit_start = expert_ids * FF + block_index * block_units
            row_at = (
                unit_start // own_units * (held_experts * CAP)
                + unit_start % own_units // block_units * CAP
                + slot_of
            )
            summed = summed + flat_rows[row_at].astype(jnp.float32)
        return summed

    expert_out = collect(back_out)
    layer_out = jnp.sum(gate_values[:, :, None] * expert_out, axis=1).astype(jnp.bfloat16)
    gate_grad = jnp.sum(cotangent.astype(jnp.float32)[:, None, :] * expert_out, axis=2)
    input_grad = jnp.sum(collect(back_in), axis=1).astype(jnp.bfloat16)
    x_columns = jnp.transpose(rows_x, (2, 0, 1))
    d_columns = jnp.transpose(rows_d, (2, 0, 1))
    grad_in_part = (
        jnp.einsum("dkr,krf->dkf", x_columns, dhid, preferred_element_type=jnp.float32).reshape(
            model_width, own_units
        )
        * factor
    )
    grad_out_part = (
        jnp.einsum("dkr,krf->dkf", d_columns, act, preferred_element_type=jnp.float32).reshape(
            model_width, own_units
        )
        * factor
    )
    summed_grads = lax.psum_scatter(
        jnp.concatenate([grad_in_part, grad_out_part], axis=1).astype(jnp.bfloat16),
        "dp",
        scatter_dimension=0,
        tiled=True,
    ).astype(jnp.float32)
    weight_in_grad = summed_grads[:, :own_units]
    weight_out_grad = summed_grads[:, own_units:]
    return (layer_out, gate_grad, input_grad, weight_in_grad, weight_out_grad)


def local(tokens, gate_values, expert_ids, cotangent, weight_in, weight_out):
    units = weight_in.shape[0]
    sources, groups = lax.axis_size("seq"), lax.axis_size("dp")
    row_values = sources * max(units // FF, 1) * CAP * groups
    paired = sources & (sources - 1) == 0 and groups & (groups - 1) == 0 and groups > 1
    plan = local_rows if units % FF == 0 and row_values < units and paired else local_sums
    return plan(tokens, gate_values, expert_ids, cotangent, weight_in, weight_out)


def solution(mesh):
    in_specs = (
        P(("dp", "seq"), None),
        P(("dp", "seq"), None),
        P(("dp", "seq"), None),
        P(("dp", "seq"), None),
        P("seq", None),
        P("seq", None),
    )
    out_specs = (
        P(("dp", "seq"), None),
        P(("dp", "seq"), None),
        P(("dp", "seq"), None),
        P("dp", "seq"),
        P("dp", "seq"),
    )
    return jax.shard_map(local, mesh=mesh, in_specs=in_specs, out_specs=out_specs, check_vma=False)
```

```python
import functools

import jax
import jax.numpy as jnp
import numpy as np
from jax import lax
from jax.experimental import pallas as pl
from jax.experimental.pallas import tpu as pltpu
from jax.sharding import PartitionSpec as P

E = 32
FF = 1024
CAP = 9

BF16 = jnp.bfloat16
F32 = jnp.float32

gelu_scale = 0.7978845608028654
gelu_cubic = 0.044715


def gelu_value(values):
    inner_arg = gelu_scale * (values + gelu_cubic * values * values * values)
    return 0.5 * values * (1.0 + jnp.tanh(inner_arg))


def gelu_slope(values):
    inner_arg = gelu_scale * (values + gelu_cubic * values * values * values)
    tanh_val = jnp.tanh(inner_arg)
    return 0.5 * (1.0 + tanh_val) + 0.5 * values * (1.0 - tanh_val * tanh_val) * gelu_scale * (
        1.0 + 3.0 * gelu_cubic * values * values
    )


def gelu_both(values):
    square = values * values
    tanh_val = jnp.tanh(gelu_scale * (values + gelu_cubic * square * values))
    half_up = 0.5 * (1.0 + tanh_val)
    slope = half_up + 0.5 * values * (1.0 - tanh_val * tanh_val) * gelu_scale * (
        1.0 + 3.0 * gelu_cubic * square
    )
    return values * half_up, slope


def iota(shape, dim):
    return lax.broadcasted_iota(jnp.int32, shape, dim)


def quotient(numbers, divisor):
    return jnp.floor((numbers.astype(F32) + 0.5) * (1.0 / divisor)).astype(jnp.int32)


def dot(a, b, dims):
    return lax.dot_general(a, b, ((dims[0], dims[1]), ((), ())), preferred_element_type=F32)


def ones_where(mask):
    return jnp.where(mask, 1.0, 0.0).astype(BF16)


def slab_slot(numbers, slots):
    slab = quotient(numbers, 2 * slots)
    rest = numbers - slab * (2 * slots)
    right = rest >= slots
    return slab, jnp.where(right, rest - slots, rest), right


def here(axis):
    return lax.axis_index(axis).astype(jnp.int32)


def token_kernel(slots, sources, ids_hbm, gate_hbm, tok_hbm, *refs):
    slab_refs, (target_ref, ids_ref, gate_ref, tok_ref, sems) = refs[: sources - 1], refs[sources - 1 :]
    gate_copy = pltpu.make_async_copy(gate_hbm, gate_ref, sems.at[2])
    ids_copy = pltpu.make_async_copy(ids_hbm, ids_ref, sems.at[0])
    tok_copy = pltpu.make_async_copy(tok_hbm, tok_ref, sems.at[1])
    ids_copy.start()
    tok_copy.start()
    gate_copy.start()
    count = tok_ref.shape[0]
    half = tok_ref.shape[1] // 2
    expert = iota((E, count), 0)
    earlier = ones_where(iota((count, count), 0) < iota((count, count), 1))
    slab, slot, right = slab_slot(iota((sources * 2 * slots, 1), 0), slots)
    slot = (slab ^ here("seq")) * slots + slot
    ids_copy.wait()
    ids = ids_ref[...]
    first, second = ids[0:1, :], ids[1:2, :]
    hot_first, hot_second = expert == first, expert == second
    before = dot(ones_where(hot_first | hot_second), earlier, ((1,), (0,)))
    slot_first = jnp.sum(jnp.where(hot_first, before, 0.0), axis=0, keepdims=True)
    slot_second = jnp.sum(jnp.where(hot_second, before, 0.0), axis=0, keepdims=True)
    target_first = first * CAP + slot_first.astype(jnp.int32)
    target_second = second * CAP + slot_second.astype(jnp.int32)
    gate_copy.wait()
    target_ref[0:1, :] = target_first.astype(F32)
    target_ref[1:2, :] = target_second.astype(F32)
    target_ref[2:4, :] = gate_ref[...]
    pick = ones_where((slot == target_first) | (slot == target_second))
    tok_copy.wait()
    rows = dot(pick, tok_ref[...], ((1,), (0,)))
    rows = jnp.where(right, rows[:, half:], rows[:, :half]).astype(BF16)
    for j, slab_ref in enumerate(slab_refs):
        slab_ref[...] = rows[(j + 1) * 2 * slots : (j + 2) * 2 * slots]


def cotangent_kernel(slots, mask, target_ref, cot_ref, tok_ref, slab_ref, own_ref):
    half = cot_ref.shape[1] // 2
    targets = target_ref[0:2, :].astype(jnp.int32)
    slab, slot, right = slab_slot(iota((slab_ref.shape[0], 1), 0), slots)
    slot = (slab ^ mask) * slots + slot
    is_first, is_second = slot == targets[0:1, :], slot == targets[1:2, :]
    gate = jnp.sum(
        jnp.where(is_first, target_ref[2:3, :], 0.0) + jnp.where(is_second, target_ref[3:4, :], 0.0),
        axis=1,
        keepdims=True,
    )
    rows = dot(ones_where(is_first | is_second), cot_ref[...], ((1,), (0,)))
    slab_ref[...] = (jnp.where(right, rows[:, half:], rows[:, :half]) * gate).astype(BF16)
    slab, slot, right = slab_slot(iota((own_ref.shape[0], 1), 0), slots)
    slot = here("seq") * slots + slot
    pick = ones_where((slot == targets[0:1, :]) | (slot == targets[1:2, :]))
    rows = dot(pick, tok_ref[...], ((1,), (0,)))
    own_ref[...] = jnp.where(right, rows[:, half:], rows[:, :half]).astype(BF16)


def regroup_kernel(slots, held, sources, mask, *refs):
    slab_refs, rows_ref = refs[:-1], refs[-1]
    per_expert = sources * CAP
    half = slab_refs[0].shape[1]
    number = iota((held * per_expert, 1), 0)
    expert = quotient(number, per_expert)
    rest = number - expert * per_expert
    source = quotient(rest, CAP)
    slab = source ^ (here("seq") if len(slab_refs) > 1 else mask)
    row = slab * (2 * slots) + expert * CAP + rest - source * CAP
    at = iota((held * per_expert, 2 * slots * sources), 1)
    slabs = jnp.concatenate([ref[...] for ref in slab_refs], axis=0)
    for side in (0, 1):
        rows = dot(ones_where(at == row + side * slots), slabs, ((1,), (0,)))
        for k in range(held):
            span = slice(k * per_expert, (k + 1) * per_expert)
            rows_ref[k, :, side * half : (side + 1) * half] = rows[span].astype(BF16)


def send_slabs(parts, slots, held, sources, mask, out_hbm, out_ref, sems):
    per_expert = sources * CAP
    rows = jnp.concatenate(parts, axis=0).astype(BF16)
    half = rows.shape[1] // 2
    size = slots * sources
    copies = []
    for piece in (0, 1):
        span = pl.ds(piece * size, size)
        source, slot, right = slab_slot(iota((size, 1), 0) + piece * size, slots)
        expert = quotient(slot, CAP)
        row = expert * per_expert + (source ^ mask) * CAP + slot - expert * CAP
        out = dot(ones_where(iota((size, held * per_expert), 1) == row), rows, ((1,), (0,)))
        out_ref[span] = jnp.where(right, out[:, half:], out[:, :half]).astype(BF16)
        copies.append(pltpu.make_async_copy(out_ref.at[span], out_hbm.at[span], sems.at[piece]))
        copies[piece].start()
    return copies


def loads_of(sources_and_targets, sems):
    copies = []
    for i, (there, near) in enumerate(sources_and_targets):
        copies.append([pltpu.make_async_copy(there.at[k], near.at[k], sems.at[i, k]) for k in range(near.shape[0])])
        for copy in copies[i]:
            copy.start()
    return copies


def forward_kernel(slots, held, sources, mask, rows_hbm, up_hbm, down_hbm, out_hbm, act_hbm, slope_hbm, *scratch):
    rows_ref, up_ref, down_ref, act_ref, slope_ref, out_ref, sems = scratch
    own, ups, downs = loads_of([(rows_hbm, rows_ref), (up_hbm, up_ref), (down_hbm, down_ref)], sems)
    stores = []

    for k in range(held):
        own[k].wait()
        ups[k].wait()
        value, slope = gelu_both(dot(rows_ref[k], up_ref[k], ((1,), (1,))))
        act_ref[k] = value.astype(BF16)
        slope_ref[k] = slope.astype(BF16)
        for i, (near, there) in enumerate([(act_ref, act_hbm), (slope_ref, slope_hbm)]):
            stores.append(pltpu.make_async_copy(near.at[k], there.at[k], sems.at[3 + i, k]))
            stores[-1].start()
    parts = []
    for k in range(held):
        downs[k].wait()
        parts.append(dot(act_ref[k], down_ref[k], ((1,), (0,))))
    stores = stores + send_slabs(parts, slots, held, sources, mask, out_hbm, out_ref, sems.at[5])
    for store in stores:
        store.wait()


def backward_kernel(slots, held, sources, mask, rows_hbm, slope_hbm, up_hbm, down_hbm, out_hbm, dhid_hbm, *scratch):
    rows_ref, up_ref, down_ref, dhid_ref, slope_ref, out_ref, sems = scratch
    own, slopes, ups, downs = loads_of(
        [(rows_hbm, rows_ref), (slope_hbm, slope_ref), (up_hbm, up_ref), (down_hbm, down_ref)], sems
    )
    stores = []
    for k in range(held):
        own[k].wait()
        slopes[k].wait()
        ups[k].wait()
        back = dot(rows_ref[k], up_ref[k], ((1,), (1,)))
        dhid_ref[k] = (back * slope_ref[k].astype(F32)).astype(BF16)
        stores.append(pltpu.make_async_copy(dhid_ref.at[k], dhid_hbm.at[k], sems.at[4, k]))
        stores[-1].start()
    parts = []
    for k in range(held):
        downs[k].wait()
        parts.append(dot(dhid_ref[k], down_ref[k], ((1,), (0,))))
    stores = stores + send_slabs(parts, slots, held, sources, mask, out_hbm, out_ref, sems.at[5])
    for store in stores:
        store.wait()


def gradient_kernel(peers, factor, share_ref, *refs):
    own_x_ref, own_d_ref, act_ref, dhid_ref, up_ref, down_ref = refs[:6]
    x_refs, d_refs = refs[6 : 6 + peers], refs[6 + peers : 6 + 2 * peers]
    grad_in_ref, grad_out_ref = refs[6 + 2 * peers :]
    wide = grad_in_ref.shape[0]
    share = pl.ds(pl.multiple_of(share_ref[0] * wide, 128), wide)
    rows_x = jnp.concatenate([ref[0] for ref in x_refs], axis=0)
    rows_d = jnp.concatenate([ref[0] for ref in d_refs], axis=0)
    hidden = dot(rows_x, up_ref[0], ((1,), (1,)))
    back = dot(rows_d, down_ref[0], ((1,), (1,)))
    value, slope = gelu_both(hidden)
    acts = jnp.concatenate([act_ref[0], value.astype(BF16)], axis=0)
    cut_d = jnp.concatenate([own_d_ref[0]] + [ref[0, :, share] for ref in d_refs], axis=0)
    grad_out_ref[...] = dot(cut_d, acts, ((0,), (0,))) * factor
    dhids = jnp.concatenate([dhid_ref[0], (back * slope).astype(BF16)], axis=0)
    cut_x = jnp.concatenate([own_x_ref[0]] + [ref[0, :, share] for ref in x_refs], axis=0)
    grad_in_ref[...] = dot(cut_x, dhids, ((0,), (0,))) * factor


def as_column(row):
    count = row.shape[1]
    same = iota((count, count), 0) == iota((count, count), 1)
    return jnp.sum(jnp.where(same, row, 0.0), axis=1, keepdims=True)


def as_row(column):
    count = column.shape[0]
    same = iota((count, count), 0) == iota((count, count), 1)
    return jnp.sum(jnp.where(same, column, 0.0), axis=0, keepdims=True)


def picked(target_ref, slots, rows, mask):
    slab, slot, right = slab_slot(iota((1, rows), 1), slots)
    slot = (slab ^ mask) * slots + slot
    columns = [as_column(target_ref[k : k + 1, :]).astype(jnp.int32) for k in (0, 1)]
    return [[(slot == column) & ~right, (slot == column) & right] for column in columns]


def combine_kernel(slots, mask, target_ref, cot_ref, out_ref, in_ref, layer_ref, gate_grad_ref, input_ref):
    half = out_ref.shape[1]
    picks = picked(target_ref, slots, out_ref.shape[0], mask)
    outs, ins = out_ref[...], in_ref[...]
    gates = target_ref[2:4, :]
    cot = cot_ref[...].astype(F32)
    count = cot.shape[0]
    columns = [as_column(gates[k : k + 1, :]) for k in (0, 1)]
    layer, grads = [], [0.0, 0.0]
    for side in (0, 1):
        both = jnp.concatenate([ones_where(picks[k][side]) for k in (0, 1)], axis=0)
        both = dot(both, outs, ((1,), (0,)))
        rows = [both[:count], both[count:]]
        layer.append(columns[0] * rows[0] + columns[1] * rows[1])
        part = cot[:, side * half : (side + 1) * half]
        for k in (0, 1):
            grads[k] = grads[k] + jnp.sum(part * rows[k], axis=1, keepdims=True)
    dots = [as_row(grad) for grad in grads]
    gate_grad_ref[...] = jnp.concatenate(dots, axis=0)
    for side in (0, 1):
        span = slice(side * half, (side + 1) * half)
        layer_ref[:, span] = layer[side].astype(BF16)
        pick = ones_where(picks[0][side] | picks[1][side])
        input_ref[:, span] = dot(pick, ins, ((1,), (0,))).astype(BF16)


def params(mib=58):
    return pltpu.CompilerParams(vmem_limit_bytes=mib * 1024 * 1024)


def cost(flops, bytes_accessed):
    return pl.CostEstimate(flops=int(flops), bytes_accessed=int(bytes_accessed), transcendentals=0)


def local_rows(tokens, gate_values, expert_ids, cotangent, weight_in, weight_out):
    sources = lax.axis_size("seq")
    groups = lax.axis_size("dp")
    peers = groups - 1
    count, width = tokens.shape
    half = width // 2
    held = weight_in.shape[0] // FF
    slots = held * CAP
    per_expert = sources * CAP
    stacked = sources * 2 * slots
    factor = (E / (2.0 * count * sources * groups)) ** 0.5
    slab = jax.ShapeDtypeStruct((stacked, half), BF16)
    mask = sources // 4
    rows_shape = jax.ShapeDtypeStruct((held, per_expert, width), BF16)
    units_shape = jax.ShapeDtypeStruct((held, per_expert, FF), BF16)
    peers_shape = jax.ShapeDtypeStruct((held, peers * per_expert, FF), BF16)
    product = 2 * held * per_expert * FF * width
    vmem = pl.BlockSpec(memory_space=pltpu.VMEM)

    hbm = pl.BlockSpec(memory_space=pltpu.HBM)
    sems = pltpu.SemaphoreType.DMA

    def by_expert(shape):
        return pl.BlockSpec((1, *shape), lambda k, *_: (k, 0, 0))

    ids_rows, gate_rows = expert_ids.T, gate_values.T
    piece = jax.ShapeDtypeStruct((2 * slots, half), BF16)
    *pieces, target = pl.pallas_call(
        functools.partial(token_kernel, slots, sources),
        out_shape=(piece,) * (sources - 1) + (jax.ShapeDtypeStruct((4, count), F32),),
        in_specs=[hbm] * 3,
        out_specs=(vmem,) * sources,
        scratch_shapes=[
            pltpu.VMEM((2, count), jnp.int32),
            pltpu.VMEM((2, count), F32),
            pltpu.VMEM((count, width), BF16),
            sems((3,)),
        ],
        compiler_params=params(),
        name="dispatch_tokens",
    )(ids_rows, gate_rows, tokens)
    win = weight_in.reshape(held, FF, width)
    wout = weight_out.reshape(held, FF, width)

    def exchange(stack):
        cut = stack.reshape(sources, 2 * slots, half)
        order = [[j ^ mask for j in range(sources)]]
        got = lax.all_to_all(cut, "seq", split_axis=0, concat_axis=0, tiled=True, axis_index_groups=order)
        return got.reshape(stacked, half)

    def regroup(*stacks):
        return pl.pallas_call(
            functools.partial(regroup_kernel, slots, held, sources, mask),
            out_shape=rows_shape,
            in_specs=[vmem] * len(stacks),
            out_specs=vmem,
            compiler_params=params(6),
            cost_estimate=cost(product, 4 * stacked * half),
            name="regroup",
        )(*stacks)

    def across(rows, axis, bit):
        return lax.ppermute(rows, axis, [(i, i ^ bit) for i in range(lax.axis_size(axis))])

    def from_peers(rows, first):
        got, bit = [rows, first], far // 2
        while bit:
            got = got + [across(one, "dp", bit) for one in got]
            bit = bit // 2
        return got

    far = groups // 2
    send_d, own_piece = pl.pallas_call(
        functools.partial(cotangent_kernel, slots, mask),
        out_shape=(slab, piece),
        in_specs=[vmem] * 3,
        out_specs=(vmem, vmem),
        compiler_params=params(6),
        name="dispatch_cotangents",
    )(target, cotangent, tokens)
    arrived = [own_piece] + [across(pieces[j - 1], "seq", j) for j in range(1, sources)]
    order = range(sources - 1, 0, -1)
    send_d, *moved = lax.optimization_barrier((send_d, *[arrived[j] for j in order]))
    for j, one in zip(order, moved):
        arrived[j] = one
    got_d = exchange(send_d)
    rows_x = regroup(*arrived)
    first_x = across(rows_x, "dp", far)

    units = pltpu.VMEM((held, per_expert, FF), BF16)
    experts = pltpu.VMEM((held, FF, width), BF16)
    near_rows = pltpu.VMEM((held, per_expert, width), BF16)
    near_slab = pltpu.VMEM((stacked, half), BF16)
    send_out, act, slope = pl.pallas_call(
        functools.partial(forward_kernel, slots, held, sources, mask),
        out_shape=(slab, units_shape, units_shape),
        in_specs=[hbm] * 3,
        out_specs=(hbm,) * 3,
        scratch_shapes=[near_rows, experts, experts, units, units, near_slab, sems((6, max(held, 2)))],
        compiler_params=params(),
        cost_estimate=cost(4 * product, 4 * weight_in.size),
        name="expert_forward",
    )(rows_x, win, wout)
    got_out = exchange(send_out)
    first_x, rows_x, act = lax.optimization_barrier((first_x, rows_x, act))
    rows_d = regroup(got_d)
    first_d = across(rows_d, "dp", far)
    all_x = from_peers(rows_x, first_x)
    send_in, dhid = pl.pallas_call(
        functools.partial(backward_kernel, slots, held, sources, mask),
        out_shape=(slab, units_shape),
        in_specs=[hbm] * 4,
        out_specs=(hbm,) * 2,
        scratch_shapes=[near_rows, experts, experts, units, units, near_slab, sems((6, max(held, 2)))],
        compiler_params=params(),
        cost_estimate=cost(4 * product, 4 * weight_in.size),
        name="expert_backward",
    )(rows_d, slope, wout, win)
    first_d, rows_d, dhid = lax.optimization_barrier((first_d, rows_d, dhid))
    got_in = exchange(send_in)
    all_d = from_peers(rows_d, first_d)

    share = width // groups
    index = lax.axis_index("dp").astype(jnp.int32).reshape(1)
    gradient = jax.ShapeDtypeStruct((share, held * FF), F32)
    parts = 1
    some = FF // parts
    gradient_spec = pl.BlockSpec((share, some), lambda k, f, index: (0, k * parts + f))
    cut = pl.BlockSpec((1, per_expert, share), lambda k, f, index: (k, 0, index[0]))
    full = pl.BlockSpec((1, per_expert, width), lambda k, f, index: (k, 0, 0))
    own = pl.BlockSpec((1, per_expert, some), lambda k, f, index: (k, 0, f))
    weights = pl.BlockSpec((1, some, width), lambda k, f, index: (k, f, 0))
    weight_in_grad, weight_out_grad = pl.pallas_call(
        functools.partial(gradient_kernel, peers, factor),
        out_shape=(gradient, gradient),
        grid_spec=pltpu.PrefetchScalarGridSpec(
            num_scalar_prefetch=1,
            grid=(held, parts),
            in_specs=[cut, cut, own, own, weights, weights] + [full] * (2 * peers),
            out_specs=(gradient_spec, gradient_spec),
        ),
        compiler_params=params(),
        cost_estimate=cost(12 * product, 8 * weight_in.size),
        name="gradients",
    )(index, rows_x, rows_d, act, dhid, win, wout, *all_x[1:], *all_d[1:])

    got_in, got_out, weight_in_grad = lax.optimization_barrier((got_in, got_out, weight_in_grad))
    token_shape = jax.ShapeDtypeStruct((count, width), BF16)
    layer_out, gate_grad, input_grad = pl.pallas_call(
        functools.partial(combine_kernel, slots, mask),
        out_shape=(token_shape, jax.ShapeDtypeStruct((2, count), F32), token_shape),
        in_specs=[vmem] * 4,
        out_specs=(vmem,) * 3,
        compiler_params=params(6),
        name="combine",
    )(target, cotangent, got_out, got_in)
    return layer_out, gate_grad.T, input_grad, weight_in_grad, weight_out_grad


def slot_numbers(ids_block):
    flat_ids = ids_block.reshape(-1)
    onehot = (flat_ids[:, None] == jnp.arange(E, dtype=jnp.int32)[None, :]).astype(jnp.int32)
    before = jnp.cumsum(onehot, axis=0) - onehot
    return jnp.sum(before * onehot, axis=1).reshape(ids_block.shape)


def local_sums(tokens, gate_values, expert_ids, cotangent, weight_in, weight_out):
    seq_count = lax.axis_size("seq")
    group_count = lax.axis_size("dp")
    own_units = weight_in.shape[0]
    block_units = min(FF, own_units)
    held_experts = own_units // block_units
    block_count = FF // block_units
    tok_count = tokens.shape[0]
    model_width = tokens.shape[1]
    factor = (E / (2.0 * tok_count * seq_count * group_count)) ** 0.5
    row_total = seq_count * CAP
    slot_of = slot_numbers(expert_ids)
    flat_target = (expert_ids * CAP + slot_of).reshape(-1)
    token_of = jnp.repeat(jnp.arange(tok_count, dtype=jnp.int32), 2)
    slot_token = jnp.zeros((E * CAP,), jnp.int32).at[flat_target].set(token_of)
    slot_used = jnp.zeros((E * CAP,), jnp.float32).at[flat_target].set(1.0)
    slot_gate = jnp.zeros((E * CAP,), jnp.float32).at[flat_target].set(gate_values.reshape(-1))
    column = np.arange(seq_count * held_experts * CAP)
    owner_of = column // (held_experts * CAP)
    local_of = column // CAP % held_experts
    expert_of = (owner_of * own_units + local_of * block_units) // FF
    code_table = jnp.asarray(expert_of * CAP + column % CAP, dtype=jnp.int32)
    col_token = slot_token[code_table]
    col_used = slot_used[code_table]
    col_gate = slot_gate[code_table]
    send_shape = (seq_count, held_experts * CAP, model_width)
    send_x = (
        (tokens[col_token].astype(jnp.float32) * col_used[:, None])
        .astype(jnp.bfloat16)
        .reshape(send_shape)
    )
    send_d = (
        (cotangent[col_token].astype(jnp.float32) * col_gate[:, None])
        .astype(jnp.bfloat16)
        .reshape(send_shape)
    )
    win_local = weight_in.reshape(held_experts, block_units, model_width)
    wout_local = weight_out.reshape(held_experts, block_units, model_width)

    def to_rows(arrived):
        grouped = arrived.reshape(seq_count, held_experts, CAP, model_width)
        return jnp.transpose(grouped, (1, 0, 2, 3)).reshape(held_experts, row_total, model_width)

    def from_rows(results):
        grouped = results.reshape(held_experts, seq_count, CAP, model_width)
        return jnp.transpose(grouped, (1, 0, 2, 3)).reshape(send_shape)

    rows_x = to_rows(lax.all_to_all(send_x, "seq", split_axis=0, concat_axis=0, tiled=True))
    hidden = jnp.einsum("krd,kfd->krf", rows_x, win_local, preferred_element_type=jnp.float32)
    act = gelu_value(hidden).astype(jnp.bfloat16)
    part_out = jnp.einsum(
        "krf,kfd->krd", act, wout_local, preferred_element_type=jnp.float32
    ).astype(jnp.bfloat16)
    back_out = lax.all_to_all(from_rows(part_out), "seq", split_axis=0, concat_axis=0, tiled=True)
    rows_d = to_rows(lax.all_to_all(send_d, "seq", split_axis=0, concat_axis=0, tiled=True))
    back_hidden = jnp.einsum("krd,kfd->krf", rows_d, wout_local, preferred_element_type=jnp.float32)
    dhid = (back_hidden * gelu_slope(hidden)).astype(jnp.bfloat16)
    part_in = jnp.einsum(
        "krf,kfd->krd", dhid, win_local, preferred_element_type=jnp.float32
    ).astype(jnp.bfloat16)
    back_in = lax.all_to_all(from_rows(part_in), "seq", split_axis=0, concat_axis=0, tiled=True)

    def collect(returned):
        flat_rows = returned.reshape(-1, model_width)
        summed = jnp.zeros((tok_count, 2, model_width), jnp.float32)
        for block_index in range(block_count):
            unit_start = expert_ids * FF + block_index * block_units
            row_at = (
                unit_start // own_units * (held_experts * CAP)
                + unit_start % own_units // block_units * CAP
                + slot_of
            )
            summed = summed + flat_rows[row_at].astype(jnp.float32)
        return summed

    expert_out = collect(back_out)
    layer_out = jnp.sum(gate_values[:, :, None] * expert_out, axis=1).astype(jnp.bfloat16)
    gate_grad = jnp.sum(cotangent.astype(jnp.float32)[:, None, :] * expert_out, axis=2)
    input_grad = jnp.sum(collect(back_in), axis=1).astype(jnp.bfloat16)
    x_columns = jnp.transpose(rows_x, (2, 0, 1))
    d_columns = jnp.transpose(rows_d, (2, 0, 1))
    grad_in_part = (
        jnp.einsum("dkr,krf->dkf", x_columns, dhid, preferred_element_type=jnp.float32).reshape(
            model_width, own_units
        )
        * factor
    )
    grad_out_part = (
        jnp.einsum("dkr,krf->dkf", d_columns, act, preferred_element_type=jnp.float32).reshape(
            model_width, own_units
        )
        * factor
    )
    summed_grads = lax.psum_scatter(
        jnp.concatenate([grad_in_part, grad_out_part], axis=1).astype(jnp.bfloat16),
        "dp",
        scatter_dimension=0,
        tiled=True,
    ).astype(jnp.float32)
    weight_in_grad = summed_grads[:, :own_units]
    weight_out_grad = summed_grads[:, own_units:]
    return (layer_out, gate_grad, input_grad, weight_in_grad, weight_out_grad)


def local(tokens, gate_values, expert_ids, cotangent, weight_in, weight_out):
    units = weight_in.shape[0]
    sources, groups = lax.axis_size("seq"), lax.axis_size("dp")
    row_values = sources * max(units // FF, 1) * CAP * groups
    paired = sources & (sources - 1) == 0 and groups & (groups - 1) == 0 and groups > 1
    plan = local_rows if units % FF == 0 and row_values < units and paired else local_sums
    return plan(tokens, gate_values, expert_ids, cotangent, weight_in, weight_out)


def solution(mesh):
    in_specs = (
        P(("dp", "seq"), None),
        P(("dp", "seq"), None),
        P(("dp", "seq"), None),
        P(("dp", "seq"), None),
        P("seq", None),
        P("seq", None),
    )
    out_specs = (
        P(("dp", "seq"), None),
        P(("dp", "seq"), None),
        P(("dp", "seq"), None),
        P("dp", "seq"),
        P("dp", "seq"),
    )
    return jax.shard_map(local, mesh=mesh, in_specs=in_specs, out_specs=out_specs, check_vma=False)
```
